32 devices in a mesh: dp: 8 (over z, y), blk: 2 (over core), uly: 2 (over x).
Axes of the slice: x: 2, y: 2, z: 4, core: 2. Of those that a mesh axis runs over, the one named last changes fastest.
Arguments:
- inputs: bfloat16 [16, 1024, 768], P('dp', ('blk', 'uly')), may hold values from -6 to 6
- cotangent: bfloat16 [16, 1024, 768], P('dp', ('blk', 'uly')), may hold values from -6 to 6
- first_gain: bfloat16 [2, 768], P(None, 'dp'), may hold values from 0.5 to 1.5
- first_shift: bfloat16 [2, 768], P(None, 'dp'), may hold values from -1 to 1
- in_weight: bfloat16 [2, 768, 2304], P(None, 'dp'), may hold values from -0.21875 to 0.21875
- query_bias: bfloat16 [2, 768], P(None, 'dp'), may hold values from -1 to 1
- value_bias: bfloat16 [2, 768], P(None, 'dp'), may hold values from -1 to 1
- out_weight: bfloat16 [2, 768, 768], P(None, 'dp'), may hold values from -0.875 to 0.875
- out_bias: bfloat16 [2, 768], P(None, 'dp'), may hold values from -1 to 1
- second_gain: bfloat16 [2, 768], P(None, 'dp'), may hold values from 0.5 to 1.5
- second_shift: bfloat16 [2, 768], P(None, 'dp'), may hold values from -1 to 1
- up_weight: bfloat16 [2, 768, 3072], P(None, 'dp'), may hold values from -0.21875 to 0.21875
- up_bias: bfloat16 [2, 3072], P(None, 'dp'), may hold values from -1 to 1
- down_weight: bfloat16 [2, 3072, 768], P(None, 'dp'), may hold values from -0.109375 to 0.109375
- down_bias: bfloat16 [2, 768], P(None, 'dp'), may hold values from -1 to 1
Outputs:
- outputs: float32 [16, 1024, 768], P('dp', ('blk', 'uly'))
- input_gradient: float32 [16, 1024, 768], P('dp', ('blk', 'uly'))
- first_gain_gradient: float32 [2, 768], P(None, 'dp')
- first_shift_gradient: float32 [2, 768], P(None, 'dp')
- in_weight_gradient: float32 [2, 768, 2304], P(None, 'dp')
- query_bias_gradient: float32 [2, 768], P(None, 'dp')
- value_bias_gradient: float32 [2, 768], P(None, 'dp')
- out_weight_gradient: float32 [2, 768, 768], P(None, 'dp')
- out_bias_gradient: float32 [2, 768], P(None, 'dp')
- second_gain_gradient: float32 [2, 768], P(None, 'dp')
- second_shift_gradient: float32 [2, 768], P(None, 'dp')
- up_weight_gradient: float32 [2, 768, 3072], P(None, 'dp')
- up_bias_gradient: float32 [2, 3072], P(None, 'dp')
- down_weight_gradient: float32 [2, 3072, 768], P(None, 'dp')
- down_bias_gradient: float32 [2, 768], P(None, 'dp')
The draws below stay inside these ranges and needn't reach their ends.
All inputs are finite; a program needn't handle non-finite values.
Results may differ from the reference program's by a relative error of at most 0.017.
Values may be sent and summed in bfloat16 or wider, within the bound.
No kernel may reach another device: no remote copies, remote signals or barrier semaphores. Data moves between devices by JAX's collectives and lax.ppermute only.
A program may use at most 256 MiB of HBM per device.

```python
import jax
import jax.numpy as jnp
from jax import lax

D = 768
FF = 3072
HEADS = 12
HDIM = 64
LAYERS = 2
LEN = 1024
SEQS = 16


def block_scale(stream_key, shape, split, least, largest):
    def one(position, parts):
        heights = jax.random.uniform(jax.random.fold_in(jax.random.fold_in(stream_key, 6), position), (parts,), jnp.float32, least / len(split), largest / len(split))
        return jnp.repeat(jnp.exp(heights), shape[position] // parts).reshape((-1,) + (1,) * (len(shape) - position - 1))

    level = one(*split[0])
    for cut in split[1:]:
        level = level * one(*cut)
    return level


def bell_draw(own_key, shape, scale, bound, shards=(), dtype=jnp.bfloat16):
    entries = jax.random.normal(own_key, shape, jnp.float32) * scale
    if len(shards) > 0:
        entries = block_scale(own_key, shape, shards, -0.22, 0.18) * entries
    return jnp.clip(entries, min=-bound, max=bound).astype(dtype)


def setup_inputs(seed: int = 0) -> dict:
    key_list = jax.random.split(jax.random.key(seed), 16)
    inputs = bell_draw(key_list[0], (SEQS, LEN, D), 1.0, 6.0, ((0, 8), (1, 4)))
    cotangent = bell_draw(key_list[1], (SEQS, LEN, D), 1.0, 6.0, ((0, 8), (1, 4)))
    first_gain = jnp.clip(1.0 + 0.1 * jax.random.normal(key_list[2], (LAYERS, D), jnp.float32), 0.5, 1.5).astype(jnp.bfloat16)
    first_shift = bell_draw(key_list[3], (LAYERS, D), 0.2, 1.0, ((1, 8),))
    in_weight = bell_draw(key_list[4], (LAYERS, D, 3 * D), D ** -0.5, 0.21875, ((1, 8),))
    query_bias = bell_draw(key_list[5], (LAYERS, D), 0.2, 1.0, ((1, 8),))
    value_bias = bell_draw(key_list[6], (LAYERS, D), 0.2, 1.0, ((1, 8),))
    out_weight = bell_draw(key_list[7], (LAYERS, D, D), (D // 16) ** -0.5, 0.875, ((1, 8),))
    out_bias = bell_draw(key_list[8], (LAYERS, D), 0.2, 1.0, ((1, 8),))
    second_gain = jnp.clip(1.0 + 0.1 * jax.random.normal(key_list[9], (LAYERS, D), jnp.float32), 0.5, 1.5).astype(jnp.bfloat16)
    second_shift = bell_draw(key_list[10], (LAYERS, D), 0.2, 1.0, ((1, 8),))
    up_weight = bell_draw(key_list[11], (LAYERS, D, FF), D ** -0.5, 0.21875, ((1, 8),))
    up_bias = bell_draw(key_list[12], (LAYERS, FF), 0.2, 1.0, ((1, 8),))
    down_weight = bell_draw(key_list[13], (LAYERS, FF, D), FF ** -0.5, 0.109375, ((1, 8),))
    down_bias = bell_draw(key_list[14], (LAYERS, D), 0.2, 1.0, ((1, 8),))
    return {"inputs": inputs, "cotangent": cotangent, "first_gain": first_gain, "first_shift": first_shift, "in_weight": in_weight, "query_bias": query_bias, "value_bias": value_bias, "out_weight": out_weight, "out_bias": out_bias, "second_gain": second_gain, "second_shift": second_shift, "up_weight": up_weight, "up_bias": up_bias, "down_weight": down_weight, "down_bias": down_bias}


@jax.custom_vjp
def low(v):
    return lax.optimization_barrier(v.astype(jnp.bfloat16)).astype(jnp.float32)

@jax.custom_vjp
def low_back(v):
    return v

def low_keep(v):
    return (low(v), None)

def low_pass(kept, grad):
    return (grad,)

def back_keep(v):
    return (v, None)

def back_low(kept, grad):
    return (low(grad),)
low.defvjp(low_keep, low_pass)
low_back.defvjp(back_keep, back_low)
EPSILON = 1e-05
NEGATIVE = -1e+30

def normalize(residual, gain, shift):
    average = lax.optimization_barrier(jnp.mean(residual, axis=-1, keepdims=True))
    centred = residual - average
    variance = lax.optimization_barrier(jnp.mean(centred * centred, axis=-1, keepdims=True))
    return centred * lax.rsqrt(variance + EPSILON) * gain + shift

def product(left, right):
    return jnp.dot(left, right, precision=lax.Precision.HIGHEST)

def attend(queries, keys, values):
    positions = jnp.arange(LEN)
    allowed = positions[None, :] <= positions[:, None]
    scores = jnp.einsum('qhd,khd->hqk', queries, keys, precision=lax.Precision.HIGHEST) * HDIM ** (-0.5)
    scores = low_back(jnp.where(allowed[None], scores, NEGATIVE))
    shares = low(jax.nn.softmax(scores, axis=-1))
    mixed = jnp.einsum('hqk,khd->qhd', shares, values, precision=lax.Precision.HIGHEST)
    return low_back(low(mixed))

def layer_forward(residual, params):
    first_gain, first_shift, in_weight, query_bias, value_bias, out_weight, out_bias, second_gain, second_shift, up_weight, up_bias, down_weight, down_bias = params
    normed = low(normalize(residual, first_gain, first_shift))
    project = product(normed, in_weight)
    queries = low_back(low(project[:, :D] + query_bias))
    keys = low_back(low(project[:, D:2 * D]))
    values = low_back(low(project[:, 2 * D:] + value_bias))
    mixed = attend(queries.reshape(LEN, HEADS, HDIM), keys.reshape(LEN, HEADS, HDIM), values.reshape(LEN, HEADS, HDIM)).reshape(LEN, D)
    middle = residual + low_back(product(mixed, out_weight)) + out_bias
    second_normed = low(normalize(middle, second_gain, second_shift))
    hidden = low_back(product(second_normed, up_weight)) + up_bias
    active = low(jax.nn.gelu(hidden, approximate=True))
    return middle + low_back(product(active, down_weight)) + down_bias

def reference(inputs, cotangent, first_gain, first_shift, in_weight, query_bias, value_bias, out_weight, out_bias, second_gain, second_shift, up_weight, up_bias, down_weight, down_bias):
    params = tuple((item.astype(jnp.float32) for item in (first_gain, first_shift, in_weight, query_bias, value_bias, out_weight, out_bias, second_gain, second_shift, up_weight, up_bias, down_weight, down_bias)))

    def forward(sequence, weights):
        residual = sequence
        for layer in range(LAYERS):
            residual = layer_forward(residual, tuple((item[layer] for item in weights)))
        return residual

    def per_sequence(totals, pair):
        sequence, incoming = pair
        result, pullback = jax.vjp(forward, sequence.astype(jnp.float32), params)
        input_slope, weight_slopes = pullback(incoming.astype(jnp.float32))
        summed = tuple((left + right for left, right in zip(totals, weight_slopes)))
        return (summed, (result, input_slope))
    zeros = tuple((jnp.zeros_like(item) for item in params))
    totals, (outputs, input_gradient) = lax.scan(per_sequence, zeros, (inputs, cotangent))
    return (outputs, input_gradient, totals[0], totals[1], totals[2], totals[3], totals[4], totals[5], totals[6], totals[7], totals[8], totals[9], totals[10], totals[11], totals[12])
```

```python
from functools import partial

import jax
import jax.numpy as jnp
from jax import lax
from jax.sharding import PartitionSpec as P

HDIM = 64
EPSILON = 1e-05
NEGATIVE = -1e30
LOW = jnp.bfloat16
FULL = jnp.float32


def normalize(residual, gain, shift):
    average = jnp.mean(residual, axis=-1, keepdims=True)
    centred = residual - average
    variance = jnp.mean(centred * centred, axis=-1, keepdims=True)
    return centred * lax.rsqrt(variance + EPSILON) * gain + shift


def norm_backward(residual, gain, shift, slope):
    unused, pullback = jax.vjp(normalize, residual, gain, shift)
    return pullback(slope)


def matmul(left, right):
    return jnp.dot(left, right, preferred_element_type=FULL)


def contract(left, right):
    return jnp.einsum("std,ste->de", left, right, preferred_element_type=FULL)


def transposed(left, right):
    return jnp.einsum("ste,de->std", left, right, preferred_element_type=FULL)


def swap(item, axis, mask=1):
    count = lax.axis_size(axis)
    return lax.ppermute(item, axis, [(i, i ^ mask) for i in range(count)])


def bit_of(axis, mask=1):
    return (lax.axis_index(axis) & mask) != 0


def ordered(own, other, bit, axis):
    low = jnp.where(bit, other, own)
    high = jnp.where(bit, own, other)
    return jnp.stack([low, high], axis=axis)


def masks_of(axis):
    count = lax.axis_size(axis)
    masks = []
    mask = 1
    while mask < count:
        masks.append(mask)
        mask *= 2
    return masks


def gather_rows(piece):
    held = piece[None]
    for mask in reversed(masks_of("dp")):
        other = swap(held, "dp", mask)
        held = ordered(held, other, bit_of("dp", mask), 1)
        held = held.reshape((-1,) + piece.shape)
    return held


def gather_axis(piece, axis):
    return ordered(piece, swap(piece, axis), bit_of(axis), 0)


def added(left, right, dtype=LOW):
    return (left.astype(FULL) + right.astype(FULL)).astype(dtype)


def halve(held, axis, mask, position):
    index = bit_of(axis, mask).astype(jnp.int32)
    keep = lax.dynamic_index_in_dim(held, index, position, keepdims=False)
    send = lax.dynamic_index_in_dim(held, 1 - index, position, keepdims=False)
    return added(keep, swap(send, axis, mask), held.dtype)


def reduce_rows(held):
    for mask in masks_of("dp"):
        held = held.reshape((-1, 2) + held.shape[1:])
        held = halve(held, "dp", mask, 1)
    return held[0]


def gather_quarters(block):
    quarter = 2 * lax.axis_index("blk") + lax.axis_index("uly")
    width = block.shape[1] // 4
    piece = lax.dynamic_slice_in_dim(block, quarter * width, width, 1)
    rows = gather_rows(piece).reshape(-1, width)
    pair = gather_axis(rows, "uly")
    return gather_axis(pair, "blk").reshape(4, -1, width)


def reduce_quarters(slopes):
    count = lax.axis_size("dp")
    four, rows, width = slopes.shape
    held = halve(slopes.reshape(2, 2, rows, width), "blk", 1, 0)
    held = halve(held, "uly", 1, 0)
    held = reduce_rows(held.reshape(count, rows // count, width))
    pair = gather_axis(held, "uly")
    every = gather_axis(pair, "blk").reshape(4, rows // count, width)
    return every.astype(FULL)


def gather_halves(block):
    width = block.shape[1] // 2
    piece = lax.dynamic_slice_in_dim(block, lax.axis_index("blk") * width, width, 1)
    rows = gather_rows(piece).reshape(-1, width)
    return rows, swap(rows, "blk")


def reduce_halves(own, other):
    count = lax.axis_size("dp")
    rows, width = own.shape
    held = added(own, swap(other, "blk"))
    held = reduce_rows(held.reshape(count, rows // count, width))
    held = added(held, swap(held, "uly"))
    pair = gather_axis(held, "blk")
    return jnp.concatenate([pair[0], pair[1]], axis=1).astype(FULL)


def reduce_small(terms):
    count = lax.axis_size("dp")
    kinds, width = terms.shape
    held = terms.reshape(kinds, count, width // count).transpose(1, 0, 2)
    held = held + swap(held, "blk")
    held = held + swap(held, "uly")
    return reduce_rows(held)


def causal_mask(length):
    query_rows = lax.broadcasted_iota(jnp.int32, (length, length), 0)
    key_rows = lax.broadcasted_iota(jnp.int32, (length, length), 1)
    return key_rows <= query_rows


def scores_for(queries, keys):
    scores = jnp.einsum("qhd,khd->hqk", queries, keys, preferred_element_type=FULL) * HDIM ** (-0.5)
    return jnp.where(causal_mask(queries.shape[0])[None], scores, NEGATIVE)


def attend(queries, keys, values):
    count = queries.shape[0]
    queries, keys, values = (item.reshape(count, -1, HDIM) for item in (queries, keys, values))
    scores = scores_for(queries, keys)
    top = jnp.max(scores, axis=-1, keepdims=True)
    raised = jnp.exp(scores - top)
    total = jnp.sum(raised, axis=-1, keepdims=True)
    shares = (raised / total).astype(LOW)
    mixed = jnp.einsum("hqk,khd->qhd", shares, values, preferred_element_type=FULL)
    return mixed.astype(LOW).reshape(count, -1), (top + jnp.log(total))[..., 0]


def attend_back(queries, keys, values, logsum, upstream):
    count = queries.shape[0]
    queries, keys, values, upstream = (
        item.reshape(count, -1, HDIM) for item in (queries, keys, values, upstream)
    )
    scale = HDIM ** (-0.5)
    shares = jnp.exp(scores_for(queries, keys) - logsum[..., None])
    against = jnp.einsum("qhd,khd->hqk", upstream, values, preferred_element_type=FULL)
    inner = jnp.sum(shares * against, axis=-1, keepdims=True)
    slopes = (shares * (against - inner)).astype(LOW)
    query_slope = jnp.einsum("hqk,khd->qhd", slopes, keys, preferred_element_type=FULL) * scale
    key_slope = jnp.einsum("hqk,qhd->khd", slopes, queries, preferred_element_type=FULL) * scale
    value_slope = jnp.einsum(
        "hqk,qhd->khd", shares.astype(LOW), upstream, preferred_element_type=FULL
    )
    return tuple(
        item.astype(LOW).reshape(count, -1) for item in (query_slope, key_slope, value_slope)
    )


def to_heads(parts):
    core = lax.axis_index("blk")
    half = parts[0].shape[-1] // 2
    mine = jnp.stack([lax.dynamic_slice_in_dim(p, core * half, half, 2) for p in parts])
    theirs = jnp.stack([lax.dynamic_slice_in_dim(p, (1 - core) * half, half, 2) for p in parts])
    joined = ordered(mine, swap(theirs, "blk"), bit_of("blk"), 2)
    joined = joined.reshape(joined.shape[:2] + (-1, half))
    return tuple(joined[i] for i in range(len(parts)))


def to_tokens(parts):
    core = lax.axis_index("blk")
    rows = parts[0].shape[1] // 2
    mine = jnp.stack([lax.dynamic_slice_in_dim(p, core * rows, rows, 1) for p in parts])
    theirs = jnp.stack([lax.dynamic_slice_in_dim(p, (1 - core) * rows, rows, 1) for p in parts])
    other = swap(theirs, "blk")
    bit = bit_of("blk")
    low = jnp.where(bit, other, mine)
    high = jnp.where(bit, mine, other)
    joined = jnp.concatenate([low, high], axis=-1)
    return tuple(joined[i] for i in range(len(parts)))


def to_sequences(local):
    place = lax.axis_index("uly")
    count, rows, width = local.shape
    paired = local.reshape(2, count // 2, rows, width)
    keep = lax.dynamic_index_in_dim(paired, place, 0, keepdims=False)
    send = lax.dynamic_index_in_dim(paired, 1 - place, 0, keepdims=False)
    joined = ordered(keep, swap(send, "uly"), bit_of("uly"), 1)
    return joined.reshape(count // 2, 2 * rows, width)


def from_sequences(held):
    place = lax.axis_index("uly")
    count, rows, width = held.shape
    paired = held.reshape(count, 2, rows // 2, width)
    keep = lax.dynamic_index_in_dim(paired, place, 1, keepdims=False)
    send = lax.dynamic_index_in_dim(paired, 1 - place, 1, keepdims=False)
    other = swap(send.astype(LOW), "uly").astype(FULL)
    joined = ordered(keep, other, bit_of("uly"), 0)
    return joined.reshape(2 * count, rows // 2, width)


def token_sum(item):
    return jnp.sum(item.astype(FULL), axis=(0, 1))


def attention_forward(residual, weights, small):
    first_gain, first_shift, query_bias, value_bias, out_bias = small[:5]
    normed = normalize(residual, first_gain, first_shift).astype(LOW)
    queries = (matmul(normed, weights[0]) + query_bias).astype(LOW)
    keys = matmul(normed, weights[1]).astype(LOW)
    values = (matmul(normed, weights[2]) + value_bias).astype(LOW)
    headed = to_heads((queries, keys, values))
    mixed, logsum = lax.map(lambda items: attend(*items), headed)
    (returned,) = to_tokens((mixed,))
    middle = residual + matmul(returned, weights[3]) + out_bias
    return middle, (normed, headed, logsum, returned)


def feed_forward(residual, up, down, small):
    second_gain, second_shift, down_bias = small[5:8]
    up_bias = small[8:12].reshape(-1)
    own, other = down
    normed = normalize(residual, second_gain, second_shift).astype(LOW)
    width = up.shape[2]
    hidden = [
        matmul(normed, up[i]) + up_bias[i * width : (i + 1) * width] for i in range(up.shape[0])
    ]
    active = jnp.concatenate(
        [jax.nn.gelu(item, approximate=True).astype(LOW) for item in hidden], axis=-1
    )
    left, right = matmul(active, own), matmul(active, other)
    bit = bit_of("blk")
    joined = jnp.concatenate([jnp.where(bit, right, left), jnp.where(bit, left, right)], axis=-1)
    return residual + joined + down_bias, (normed, hidden, active)


def feed_backward(residual, upstream, up, down, small, record):
    second_gain, second_shift = small[5:7]
    own, other = down
    normed, hidden, active = record
    down_bias_slope = token_sum(upstream)
    low_upstream = upstream.astype(LOW)
    half = own.shape[1]
    core = lax.axis_index("blk")
    mine = lax.dynamic_slice_in_dim(low_upstream, core * half, half, 2)
    theirs = lax.dynamic_slice_in_dim(low_upstream, (1 - core) * half, half, 2)
    down_slope = reduce_halves(
        contract(active, mine).astype(LOW), contract(active, theirs).astype(LOW)
    )
    active_slope = transposed(mine, own) + transposed(theirs, other)
    width = up.shape[2]
    up_bias_slopes = []
    up_slopes = []
    norm_slope = 0.0
    for i, item in enumerate(hidden):
        unused, pullback = jax.vjp(partial(jax.nn.gelu, approximate=True), item)
        hidden_slope = pullback(active_slope[..., i * width : (i + 1) * width])[0]
        up_bias_slopes.append(token_sum(hidden_slope))
        low_hidden = hidden_slope.astype(LOW)
        up_slopes.append(contract(normed, low_hidden).astype(LOW))
        norm_slope = norm_slope + transposed(low_hidden, up[i])
    up_slope = reduce_quarters(jnp.stack(up_slopes))
    residual_slope, gain_slope, shift_slope = norm_backward(
        residual, second_gain, second_shift, norm_slope
    )
    up_bias_slope = jnp.concatenate(up_bias_slopes)
    return (
        upstream + residual_slope,
        up_slope,
        down_slope,
        (gain_slope, shift_slope, down_bias_slope, up_bias_slope),
    )


def attention_backward(residual, upstream, weights, small, record):
    first_gain, first_shift = small[:2]
    normed, headed, logsum, returned = record
    out_bias_slope = token_sum(upstream)
    low_upstream = upstream.astype(LOW)
    out_slope = contract(returned, low_upstream).astype(LOW)
    mixed_slope = transposed(low_upstream, weights[3]).astype(LOW)
    (head_slope,) = to_heads((mixed_slope,))
    slopes = lax.map(lambda items: attend_back(*items), headed + (logsum, head_slope))
    parts = to_tokens(slopes)
    query_bias_slope = token_sum(parts[0])
    value_bias_slope = token_sum(parts[2])
    weight_slopes = [contract(normed, part).astype(LOW) for part in parts]
    first_slope = sum(transposed(parts[i], weights[i]) for i in range(3))
    summed = reduce_quarters(jnp.stack(weight_slopes + [out_slope]))
    residual_slope, gain_slope, shift_slope = norm_backward(
        residual, first_gain, first_shift, first_slope
    )
    return (
        upstream + residual_slope,
        summed,
        (gain_slope, shift_slope, query_bias_slope, value_bias_slope, out_bias_slope),
    )


def shards(
    inputs,
    cotangent,
    first_gain,
    first_shift,
    in_weight,
    query_bias,
    value_bias,
    out_weight,
    out_bias,
    second_gain,
    second_shift,
    up_weight,
    up_bias,
    down_weight,
    down_bias,
):
    layers, rows = in_weight.shape[0], in_weight.shape[1]
    width = out_weight.shape[2]
    vectors = jnp.stack(
        [
            first_gain,
            first_shift,
            query_bias,
            value_bias,
            out_bias,
            second_gain,
            second_shift,
            down_bias,
        ],
        axis=1,
    )
    vectors = jnp.concatenate([vectors, up_bias.reshape(layers, -1, rows)], axis=1)
    kinds = vectors.shape[1]
    gathered = gather_rows(vectors.reshape(layers * kinds, rows))
    gathered = gathered.reshape(-1, layers, kinds, rows).astype(FULL)
    straight = gathered.transpose(1, 2, 0, 3).reshape(layers, kinds, width)
    biases = gathered[:, :, 8:].transpose(1, 0, 2, 3).reshape(layers, kinds - 8, width)
    small = jnp.concatenate([straight[:, :8], biases], axis=1)

    residual = to_sequences(inputs).astype(FULL)
    records = []
    for layer in range(layers):
        weights = gather_quarters(jnp.concatenate([in_weight[layer], out_weight[layer]], axis=1))
        up = gather_quarters(up_weight[layer])
        down = gather_halves(down_weight[layer])
        entry = residual
        middle, attention_record = attention_forward(entry, weights, small[layer])
        residual, feed_record = feed_forward(middle, up, down, small[layer])
        records.append((entry, attention_record, middle, feed_record, weights, up, down))
    outputs = from_sequences(residual)
    upstream = to_sequences(cotangent).astype(FULL)
    found = [None] * layers
    for layer in reversed(range(layers)):
        entry, attention_record, middle, feed_record, weights, up, down = records[layer]
        upstream, up_slope, down_slope, feed_small = feed_backward(
            middle, upstream, up, down, small[layer], feed_record
        )
        upstream, summed, attention_small = attention_backward(
            entry, upstream, weights, small[layer], attention_record
        )
        count = lax.axis_size("dp")
        up_terms = feed_small[3].reshape(count, kinds - 8, rows).transpose(1, 0, 2)
        terms = jnp.concatenate(
            [jnp.stack(attention_small + feed_small[:3]), up_terms.reshape(kinds - 8, width)]
        )
        vectors = reduce_small(terms)
        across = summed.transpose(1, 0, 2)
        found[layer] = (
            vectors[0],
            vectors[1],
            across[:, :3].reshape(rows, 3 * width),
            vectors[2],
            vectors[3],
            across[:, 3],
            vectors[4],
            vectors[5],
            vectors[6],
            up_slope.transpose(1, 0, 2).reshape(rows, -1),
            vectors[8:].reshape(-1),
            down_slope,
            vectors[7],
        )
    input_gradient = from_sequences(upstream)
    stacked = tuple(jnp.stack([item[index] for item in found]) for index in range(13))
    return (outputs, input_gradient) + stacked


def solution(mesh):
    token = P("dp", ("blk", "uly"), None)
    vector = P(None, "dp")
    matrix = P(None, "dp", None)
    params = (
        vector,
        vector,
        matrix,
        vector,
        vector,
        matrix,
        vector,
        vector,
        vector,
        matrix,
        vector,
        matrix,
        vector,
    )
    specs = (token, token) + params
    return jax.shard_map(shards, mesh=mesh, in_specs=specs, out_specs=specs, check_vma=False)
```

```python
import jax
import jax.numpy as jnp
from jax import lax
from jax.experimental import pallas as pl
from jax.experimental.pallas import tpu as pltpu
from jax.sharding import PartitionSpec as P

HDIM = 64
EPSILON = 1e-05
NEGATIVE = -1e30
LOW = jnp.bfloat16
FULL = jnp.float32
SCALE = HDIM**-0.5
TILE = 256
MIB = 2**20


def dot_nt(left, right):
    return lax.dot_general(left, right, (((1,), (1,)), ((), ())), preferred_element_type=FULL)


def dot_nn(left, right):
    return lax.dot_general(left, right, (((1,), (0,)), ((), ())), preferred_element_type=FULL)


def head_lanes(item, head):
    lane = lax.broadcasted_iota(jnp.int32, item.shape, 1)
    return jnp.where((lane // HDIM) == head, item, jnp.zeros_like(item))


def keep_diagonal(scores):
    keys = lax.broadcasted_iota(jnp.int32, scores.shape, 0)
    rows = lax.broadcasted_iota(jnp.int32, scores.shape, 1)
    return jnp.where(keys <= rows, scores, NEGATIVE)


def join(core, mine, theirs, whole):
    half = mine.shape[0]

    @pl.when(core == 0)
    def _():
        whole[:half] = mine[...]
        whole[half:] = theirs[...]

    @pl.when(core != 0)
    def _():
        whole[:half] = theirs[...]
        whole[half:] = mine[...]


def part(core, whole, mine, theirs):
    half = mine.shape[0]

    @pl.when(core == 0)
    def _():
        mine[...] = whole[:half].astype(mine.dtype)
        theirs[...] = whole[half:].astype(theirs.dtype)

    @pl.when(core != 0)
    def _():
        theirs[...] = whole[:half].astype(theirs.dtype)
        mine[...] = whole[half:].astype(mine.dtype)


def attend_kernel(core_ref, mine_ref, theirs_ref, mixed_mine, mixed_theirs, logsum_ref, qkv, mixed_ref):
    core = core_ref[0]
    for kind in range(3):
        join(core, mine_ref.at[kind, 0], theirs_ref.at[kind, 0], qkv.at[kind])
    length = qkv.shape[1]
    values_t = qkv[2].T
    for start in range(0, length, TILE):
        rows = slice(start, start + TILE)
        queries = qkv[0, rows] * jnp.asarray(SCALE, LOW)
        outs = []
        for head in range(2):
            own = head_lanes(queries, head)
            scores = keep_diagonal(dot_nt(qkv[1, rows], own))
            top = jnp.max(scores, axis=0, keepdims=True)
            if start:
                early = dot_nt(qkv[1, :start], own)
                top = jnp.maximum(top, jnp.max(early, axis=0, keepdims=True))
            raised = jnp.exp(scores - top)
            total = jnp.sum(raised, axis=0, keepdims=True)
            mixed = dot_nn(values_t[:, rows], raised.astype(LOW))
            if start:
                raised = jnp.exp(early - top)
                total = total + jnp.sum(raised, axis=0, keepdims=True)
                mixed = mixed + dot_nn(values_t[:, :start], raised.astype(LOW))
            outs.append((mixed / total)[head * HDIM : (head + 1) * HDIM])
            logsum_ref[0, 0, head : head + 1, rows] = top + jnp.log(total)
        mixed_ref[rows] = jnp.concatenate(outs, axis=0).T.astype(LOW)
    part(core, mixed_ref, mixed_mine.at[0], mixed_theirs.at[0])


def attend(core, mine, theirs):
    three, count, rows, width = mine.shape
    pairs = width // 128
    wide = pl.BlockSpec((3, 1, rows, 128), lambda s, p, core: (0, s, 0, p))
    thin = pl.BlockSpec((1, rows, 128), lambda s, p, core: (s, 0, p))
    return pl.pallas_call(
        attend_kernel,
        grid_spec=pltpu.PrefetchScalarGridSpec(
            num_scalar_prefetch=1,
            grid=(count, pairs),
            in_specs=[wide, wide],
            out_specs=[
                thin,
                thin,
                pl.BlockSpec((1, 1, 8, 2 * rows), lambda s, p, core: (s, p, 0, 0)),
            ],
            scratch_shapes=[pltpu.VMEM((3, 2 * rows, 128), LOW), pltpu.VMEM((2 * rows, 128), LOW)],
        ),
        out_shape=[
            jax.ShapeDtypeStruct((count, rows, width), LOW),
            jax.ShapeDtypeStruct((count, rows, width), LOW),
            jax.ShapeDtypeStruct((count, pairs, 8, 2 * rows), FULL),
        ],
        compiler_params=pltpu.CompilerParams(vmem_limit_bytes=32 * MIB),
        name="attend",
    )(core, mine, theirs)


def attend_back_kernel(
    core_ref,
    mine_ref,
    theirs_ref,
    logsum_ref,
    mixed_mine,
    mixed_theirs,
    slope_mine,
    slope_theirs,
    out_mine,
    out_theirs,
    qkv,
    mixed_ref,
    slope_ref,
    grads,
):
    core = core_ref[0]
    for kind in range(3):
        join(core, mine_ref.at[kind, 0], theirs_ref.at[kind, 0], qkv.at[kind])
    join(core, mixed_mine.at[0], mixed_theirs.at[0], mixed_ref)
    join(core, slope_mine.at[0], slope_theirs.at[0], slope_ref)
    length = qkv.shape[1]
    keys_t = qkv[1].T * jnp.asarray(SCALE, LOW)
    product = (mixed_ref[...].astype(FULL) * slope_ref[...].astype(FULL)).T
    inner = [
        jnp.sum(product[h * HDIM : (h + 1) * HDIM], axis=0, keepdims=True) for h in range(2)
    ]
    for start in range(0, length, TILE):
        rows = slice(start, start + TILE)
        queries = qkv[0, rows] * jnp.asarray(SCALE, LOW)
        slope = slope_ref[rows]
        query_slopes = []
        for head in range(2):
            own = head_lanes(queries, head)
            own_slope = head_lanes(slope, head)
            logsum = logsum_ref[0, 0, head : head + 1, rows]
            query_slope = None
            for first in range(0, start + TILE, TILE):
                span = slice(first, first + TILE)
                scores = dot_nt(qkv[1, span], own)
                if first == start:
                    scores = keep_diagonal(scores)
                shares = jnp.exp(scores - logsum)
                against = dot_nt(qkv[2, span], own_slope)
                slopes = (shares * (against - inner[head][:, rows])).astype(LOW)
                value_slope = dot_nn(shares.astype(LOW), own_slope)
                key_slope = dot_nn(slopes, own)
                if first == start and head == 0:
                    grads[2, span] = value_slope
                    grads[1, span] = key_slope
                else:
                    grads[2, span] += value_slope
                    grads[1, span] += key_slope
                piece = dot_nn(keys_t[:, span], slopes)
                query_slope = piece if query_slope is None else query_slope + piece
            query_slopes.append(query_slope[head * HDIM : (head + 1) * HDIM])
        grads[0, rows] = jnp.concatenate(query_slopes, axis=0).T
    for kind in range(3):
        part(core, grads.at[kind], out_mine.at[kind, 0], out_theirs.at[kind, 0])


def attend_back(core, mine, theirs, logsum, mixed, slope):
    three, count, rows, width = mine.shape
    pairs = width // 128
    wide = pl.BlockSpec((3, 1, rows, 128), lambda s, p, core: (0, s, 0, p))
    thin = pl.BlockSpec((1, rows, 128), lambda s, p, core: (s, 0, p))
    sums = pl.BlockSpec((1, 1, 8, 2 * rows), lambda s, p, core: (s, p, 0, 0))
    return pl.pallas_call(
        attend_back_kernel,
        grid_spec=pltpu.PrefetchScalarGridSpec(
            num_scalar_prefetch=1,
            grid=(count, pairs),
            in_specs=[wide, wide, sums, thin, thin, thin, thin],
            out_specs=[wide, wide],
            scratch_shapes=[
                pltpu.VMEM((3, 2 * rows, 128), LOW),
                pltpu.VMEM((2 * rows, 128), LOW),
                pltpu.VMEM((2 * rows, 128), LOW),
                pltpu.VMEM((3, 2 * rows, 128), FULL),
            ],
        ),
        out_shape=[jax.ShapeDtypeStruct(mine.shape, LOW)] * 2,
        compiler_params=pltpu.CompilerParams(vmem_limit_bytes=32 * MIB),
        name="attend_back",
    )(core, mine, theirs, logsum, *mixed, *slope)


def normalize(residual, gain, shift):
    average = jnp.mean(residual, axis=-1, keepdims=True)
    centred = residual - average
    variance = jnp.mean(centred * centred, axis=-1, keepdims=True)
    return centred * lax.rsqrt(variance + EPSILON) * gain + shift


def norm_backward(residual, gain, shift, slope):
    unused, pullback = jax.vjp(normalize, residual, gain, shift)
    return pullback(slope)


def gelu(hidden):
    return jax.nn.gelu(hidden, approximate=True)


def matmul(left, right):
    return jnp.dot(left, right, preferred_element_type=FULL)


def contract(left, right):
    return jnp.einsum("std,ste->de", left, right, preferred_element_type=FULL).astype(LOW)


def transposed(left, right):
    return jnp.einsum("ste,de->std", left, right, preferred_element_type=FULL)


def swap(item, axis, mask=1):
    count = lax.axis_size(axis)
    return lax.ppermute(item, axis, [(i, i ^ mask) for i in range(count)])


def bit_of(axis, mask=1):
    return (lax.axis_index(axis) & mask) != 0


def masks_of(axis):
    count = lax.axis_size(axis)
    masks = []
    mask = 1
    while mask < count:
        masks.append(mask)
        mask *= 2
    return masks


def ordered(own, other, bit, axis):
    low = jnp.where(bit, other, own)
    high = jnp.where(bit, own, other)
    return jnp.stack([low, high], axis=axis)


def side_by_side(own, other, bit):
    low = jnp.where(bit, other, own)
    high = jnp.where(bit, own, other)
    return jnp.concatenate([low, high], axis=-1)


def chosen(item, bit, axis):
    return lax.dynamic_index_in_dim(item, bit.astype(jnp.int32), axis, keepdims=False)


def added(left, right):
    return (left.astype(FULL) + right.astype(FULL)).astype(LOW)


class Flow:
    def __init__(self, steps):
        self.steps = steps
        self.result = None
        self.done = False
        self.flying = None
        self.waiting = None
        self.advance(None)

    def advance(self, arrived):
        try:
            self.waiting = self.steps.send(arrived)
        except StopIteration as stop:
            self.done = True
            self.waiting = None
            self.result = stop.value

    def launch(self):
        if not self.done:
            self.flying = [swap(*send) for send in self.waiting]
            self.waiting = None


def cut(live, *flows):
    flows = [flow for flow in flows if not flow.done]
    sends = [
        flow.flying if flow.flying is not None else [item[0] for item in flow.waiting]
        for flow in flows
    ]
    live, sends = lax.optimization_barrier((live, sends))
    for flow, arrays in zip(flows, sends):
        if flow.flying is not None:
            flow.flying = None
            flow.advance(arrays)
        else:
            flow.waiting = [(a,) + item[1:] for a, item in zip(arrays, flow.waiting)]
        flow.launch()
    return live


def drain(live, *flows):
    while not all(flow.done for flow in flows):
        live = cut(live, *flows)
    return live


def grown(held, other, mask, flip=None):
    bit = bit_of("dp", mask)
    if flip is not None:
        bit = bit ^ flip
    joined = ordered(held, other, bit, -3)
    return joined.reshape(held.shape[:-3] + (-1,) + held.shape[-2:])


def gather_small(piece):
    held = piece[None]
    for mask in reversed(masks_of("dp")):
        (other,) = yield [(held, "dp", mask)]
        held = grown(held, other, mask)
    return held


def rows_of(held):
    return held.reshape(held.shape[:-3] + (-1, held.shape[-1]))


def quarter_of(block):
    width = block.shape[1] // 4
    start = (2 * lax.axis_index("uly") + lax.axis_index("blk")) * width
    return lax.dynamic_slice_in_dim(block, start, width, 1)


def gather_attention(first, second):
    held = jnp.stack([quarter_of(first), quarter_of(second)])[:, None]
    masks = masks_of("dp")
    for mask in reversed(masks[1:]):
        (other,) = yield [(held, "dp", mask)]
        held = grown(held, other, mask)
    left, right = held[0], held[1]
    place = bit_of("uly")
    other_left, other_right = yield [(left, "dp", masks[0]), (right, "uly", 1)]
    left = grown(left, other_left, masks[0])
    right = ordered(right, other_right, place, 0)
    other_left, other_right = yield [(left, "uly", 1), (right, "dp", masks[0])]
    left = rows_of(ordered(left, other_left, place, 0))
    right = rows_of(grown(right, other_right, masks[0]))
    other = yield [(left, "blk", 1), (right, "blk", 1)]
    return (left, right), tuple(other)


def gather_up(block):
    width = block.shape[1] // 4
    start = (2 * lax.axis_index("blk") + lax.axis_index("uly")) * width
    held = lax.dynamic_slice_in_dim(block, start, width, 1)[None]
    for mask in reversed(masks_of("dp")):
        (other,) = yield [(held, "dp", mask)]
        held = grown(held, other, mask)
    rows = rows_of(held)
    (other,) = yield [(rows, "uly", 1)]
    own = ordered(rows, other, bit_of("uly"), 0)
    (other,) = yield [(own, "blk", 1)]
    return own, other


def gather_down(block):
    width = block.shape[1] // 2
    held = lax.dynamic_slice_in_dim(block, lax.axis_index("blk") * width, width, 1)[None]
    masks = masks_of("dp")
    for mask in reversed(masks):
        (other,) = yield [(held, "dp", mask)]
        held = grown(held, other, mask, bit_of("blk") if mask == masks[-1] else None)
    own = held.reshape(2, -1, width)
    (other,) = yield [(own, "blk", 1)]
    return own, other


def halved(held, bit):
    return chosen(held, bit, -3), chosen(held, ~bit, -3)


def split_rows(held):
    return held.reshape(held.shape[:-3] + (-1, 2) + held.shape[-2:])


def reduce_attention(own, other):
    count = lax.axis_size("dp")
    masks = masks_of("dp")
    place = bit_of("uly")
    arrived = yield [(other[0], "blk", 1), (other[1], "blk", 1)]
    left, right = added(own[0], arrived[0]), added(own[1], arrived[1])
    two, rows, width = left.shape
    left = left.reshape(2, count, rows // count, width)
    right = right.reshape(2, count, rows // count, width)
    keep_left, send_left = chosen(left, place, 0), chosen(left, ~place, 0)
    bit = bit_of("dp", masks[0])
    keep_right, send_right = halved(split_rows(right), bit)
    arrived = yield [(send_left, "uly", 1), (send_right, "dp", masks[0])]
    left, right = added(keep_left, arrived[0]), added(keep_right, arrived[1])
    keep_left, send_left = halved(split_rows(left), bit)
    keep_right, send_right = chosen(right, place, 0), chosen(right, ~place, 0)
    arrived = yield [(send_left, "dp", masks[0]), (send_right, "uly", 1)]
    held = jnp.stack([added(keep_left, arrived[0]), added(keep_right, arrived[1])])
    for mask in masks[1:]:
        keep, send = halved(split_rows(held), bit_of("dp", mask))
        (other,) = yield [(send, "dp", mask)]
        held = added(keep, other)
    held = held[:, 0]
    (other,) = yield [(held, "uly", 1)]
    held = ordered(held, other, place, 1)
    (other,) = yield [(held, "blk", 1)]
    return ordered(held, other, bit_of("blk"), 1)


def reduce_up(own, other):
    count = lax.axis_size("dp")
    place = bit_of("uly")
    (arrived,) = yield [(other, "blk", 1)]
    held = added(own, arrived)
    two, rows, width = held.shape
    keep, send = chosen(held, place, 0), chosen(held, ~place, 0)
    (arrived,) = yield [(send, "uly", 1)]
    held = added(keep, arrived).reshape(count, rows // count, width)
    for mask in masks_of("dp"):
        keep, send = halved(split_rows(held), bit_of("dp", mask))
        (arrived,) = yield [(send, "dp", mask)]
        held = added(keep, arrived)
    held = held[0]
    (arrived,) = yield [(held, "uly", 1)]
    held = ordered(held, arrived, place, 0)
    (arrived,) = yield [(held, "blk", 1)]
    every = ordered(held, arrived, bit_of("blk"), 0)
    return jnp.concatenate([every[i, j] for i in range(2) for j in range(2)], axis=-1)


def reduce_down(own, other):
    count = lax.axis_size("dp")
    masks = masks_of("dp")
    (arrived,) = yield [(other, "blk", 1)]
    held = added(own, jnp.stack([arrived[1], arrived[0]]))
    width = held.shape[2]
    held = held.reshape(count, -1, width)
    for mask in masks:
        bit = bit_of("dp", mask)
        if mask == masks[-1]:
            bit = bit ^ bit_of("blk")
        keep, send = halved(split_rows(held), bit)
        (arrived,) = yield [(send, "dp", mask)]
        held = added(keep, arrived)
    held = held[0]
    (arrived,) = yield [(held, "uly", 1)]
    held = added(held, arrived)
    (arrived,) = yield [(held, "blk", 1)]
    return side_by_side(held, arrived, bit_of("blk"))


def to_sequences(local):
    place = bit_of("uly")
    count, rows, width = local.shape
    paired = local.reshape(2, count // 2, rows, width)
    (arrived,) = yield [(chosen(paired, ~place, 0), "uly", 1)]
    joined = ordered(chosen(paired, place, 0), arrived, place, 1)
    return joined.reshape(count // 2, 2 * rows, width)


def from_sequences(held):
    place = bit_of("uly")
    count, rows, width = held.shape
    paired = held.reshape(count, 2, rows // 2, width)
    (arrived,) = yield [(chosen(paired, ~place, 1).astype(LOW), "uly", 1)]
    joined = ordered(chosen(paired, place, 1), arrived.astype(FULL), place, 0)
    return joined.reshape(2 * count, rows // 2, width)


def token_sum(item):
    return jnp.sum(item.astype(FULL), axis=(0, 1))


def halves_of(item):
    half = item.shape[-1] // 2
    core = lax.axis_index("blk")
    axis = item.ndim - 1
    return (
        lax.dynamic_slice_in_dim(item, core * half, half, axis),
        lax.dynamic_slice_in_dim(item, (1 - core) * half, half, axis),
    )


def layer_forward(residual, small, flows, coming, core):
    attention, up_flow, down_flow = flows
    first_gain, first_shift, query_bias, value_bias, out_bias = small[:5]
    second_gain, second_shift, down_bias = small[5:8]
    up_bias = small[8:].reshape(-1)
    bit = bit_of("blk")
    next_attention, next_up, next_down = coming if coming else (None, None, None)

    def with_next(*items):
        return [item for item in items if item is not None]

    own, other = attention.result
    normed = normalize(residual, first_gain, first_shift).astype(LOW)
    normed = cut(normed, up_flow, down_flow)
    query_biases, value_biases = halves_of(query_bias), halves_of(value_bias)

    def project(weights, i):
        (query, key), (value, unused) = weights
        return jnp.stack(
            [
                (matmul(normed, query) + query_biases[i]).astype(LOW),
                matmul(normed, key).astype(LOW),
                (matmul(normed, value) + value_biases[i]).astype(LOW),
            ]
        )

    away = swap(project(other, 1), "blk")
    mine = project(own, 0)
    mine, away = cut((mine, away), up_flow, down_flow, *with_next(next_attention))
    mixed_mine, mixed_theirs, logsum = attend(core, mine, away)
    mixed_mine, mixed_theirs = cut((mixed_mine, mixed_theirs), *with_next(next_attention))
    arrived = swap(mixed_theirs, "blk")
    mixed = side_by_side(mixed_mine, arrived, bit)
    columns = side_by_side(matmul(mixed, own[1][1]), matmul(mixed, other[1][1]), bit)
    middle = residual + columns + out_bias
    normed_two = normalize(middle, second_gain, second_shift).astype(LOW)
    middle, normed_two = cut(
        (middle, normed_two), up_flow, down_flow, *with_next(next_attention)
    )
    middle, normed_two = drain((middle, normed_two), up_flow)
    up_biases = halves_of(up_bias)
    width = up_flow.result[0].shape[2]
    hidden = []
    active = []
    for weights, bias in zip(up_flow.result, up_biases):
        parts = [
            matmul(normed_two, weights[i]) + bias[i * width : (i + 1) * width] for i in range(2)
        ]
        hidden.append(parts)
        active.append(jnp.concatenate([gelu(item).astype(LOW) for item in parts], axis=-1))
    active, middle = cut(
        (active, middle), down_flow, *with_next(next_attention, next_up)
    )
    active, middle = drain((active, middle), down_flow)
    down_own, down_other = down_flow.result
    left = matmul(active[0], down_own[0]) + matmul(active[1], down_own[1])
    right = matmul(active[0], down_other[1]) + matmul(active[1], down_other[0])
    result = middle + side_by_side(left, right, bit) + down_bias
    if coming:
        result = cut(result, next_attention, next_up, next_down)
        result = cut(result, next_attention)
    record = (residual, normed, mine, away, logsum, mixed_mine, mixed_theirs, mixed)
    return result, record + (middle, normed_two, hidden, active)


def layer_backward(upstream, small, weights, record, core, before):
    (own, other), (up_own, up_other), (down_own, down_other) = weights
    first_gain, first_shift = small[:2]
    second_gain, second_shift = small[5:7]
    residual, normed, mine, away, logsum, mixed_mine, mixed_theirs, mixed = record[:8]
    middle, normed_two, hidden, active = record[8:]
    bit = bit_of("blk")

    down_bias_slope = token_sum(upstream)
    low_own, low_other = halves_of(upstream.astype(LOW))
    down_slopes = [
        jnp.stack([contract(active[i], low_other) for i in range(2)]),
        jnp.stack([contract(active[i], low_own) for i in range(2)]),
    ]
    down_flow = Flow(reduce_down(down_slopes[1], down_slopes[0]))
    low_own, low_other, upstream = cut((low_own, low_other, upstream), down_flow, *before)
    active_slopes = [
        transposed(low_own, down_own[0]) + transposed(low_other, down_other[1]),
        transposed(low_own, down_own[1]) + transposed(low_other, down_other[0]),
    ]
    low_hidden = []
    bias_slopes = []
    for slope, parts in zip(active_slopes, hidden):
        width = parts[0].shape[-1]
        for i, item in enumerate(parts):
            unused, pullback = jax.vjp(gelu, item)
            hidden_slope = pullback(slope[..., i * width : (i + 1) * width])[0]
            bias_slopes.append(token_sum(hidden_slope))
            low_hidden.append(hidden_slope.astype(LOW))
    low_hidden = cut(low_hidden, down_flow, *before)
    up_bias_slope = side_by_side(
        jnp.concatenate(bias_slopes[:2]), jnp.concatenate(bias_slopes[2:]), bit
    )
    up_slopes = [
        jnp.stack([contract(normed_two, low_hidden[2 + i]) for i in range(2)]),
        jnp.stack([contract(normed_two, low_hidden[i]) for i in range(2)]),
    ]
    up_flow = Flow(reduce_up(up_slopes[1], up_slopes[0]))
    low_hidden = cut(low_hidden, up_flow)
    norm_slope = (
        transposed(low_hidden[0], up_own[0])
        + transposed(low_hidden[1], up_own[1])
        + transposed(low_hidden[2], up_other[0])
        + transposed(low_hidden[3], up_other[1])
    )
    through, second_gain_slope, second_shift_slope = norm_backward(
        middle, second_gain, second_shift, norm_slope
    )
    middle_slope = upstream + through
    middle_slope = cut(middle_slope, up_flow, *before)

    out_bias_slope = token_sum(middle_slope)
    low_own, low_other = halves_of(middle_slope.astype(LOW))
    mixed_slope = transposed(low_own, own[1][1]) + transposed(low_other, other[1][1])
    slope_own, slope_other = halves_of(mixed_slope.astype(LOW))
    slope_away = swap(slope_other, "blk")
    out_slopes = contract(mixed, low_own), contract(mixed, low_other)
    slope_own, slope_away, out_slopes = cut((slope_own, slope_away, out_slopes), *before)
    grads_mine, grads_theirs = attend_back(
        core, mine, away, logsum, (mixed_mine, mixed_theirs), (slope_own, slope_away)
    )
    grads_mine, grads_theirs, middle_slope = cut(
        (grads_mine, grads_theirs, middle_slope), down_flow, up_flow, *before
    )
    grads_away = swap(grads_theirs, "blk")
    first, second = [], []
    for grads, out_slope in zip((grads_mine, grads_away), out_slopes):
        slopes = [contract(normed, grads[i]) for i in range(3)]
        first.append(jnp.stack(slopes[:2]))
        second.append(jnp.stack([slopes[2], out_slope]))
    attention_flow = Flow(reduce_attention((first[0], second[0]), (first[1], second[1])))
    grads_mine, grads_away, middle_slope = cut(
        (grads_mine, grads_away, middle_slope), attention_flow, *before
    )
    query_bias_slope = side_by_side(token_sum(grads_mine[0]), token_sum(grads_away[0]), bit)
    value_bias_slope = side_by_side(token_sum(grads_mine[2]), token_sum(grads_away[2]), bit)
    first_slope = 0.0
    for grads, (pair, last) in ((grads_mine, own), (grads_away, other)):
        first_slope = (
            first_slope
            + transposed(grads[0], pair[0])
            + transposed(grads[1], pair[1])
            + transposed(grads[2], last[0])
        )
    through, first_gain_slope, first_shift_slope = norm_backward(
        residual, first_gain, first_shift, first_slope
    )
    upstream = middle_slope + through
    upstream = cut(upstream, attention_flow, up_flow, down_flow, *before)
    vectors = [
        first_gain_slope,
        first_shift_slope,
        query_bias_slope,
        value_bias_slope,
        out_bias_slope,
        second_gain_slope,
        second_shift_slope,
        down_bias_slope,
    ]
    terms = jnp.concatenate([jnp.stack(vectors), up_bias_slope.reshape(-1, middle.shape[-1])])
    return upstream, terms, (attention_flow, up_flow, down_flow)


def shards(
    inputs,
    cotangent,
    first_gain,
    first_shift,
    in_weight,
    query_bias,
    value_bias,
    out_weight,
    out_bias,
    second_gain,
    second_shift,
    up_weight,
    up_bias,
    down_weight,
    down_bias,
):
    layers, rows = in_weight.shape[0], in_weight.shape[1]
    width = out_weight.shape[2]
    core = lax.axis_index("blk").astype(jnp.int32).reshape(1)
    vectors = jnp.stack(
        [
            first_gain,
            first_shift,
            query_bias,
            value_bias,
            out_bias,
            second_gain,
            second_shift,
            down_bias,
        ],
        axis=1,
    )
    vectors = jnp.concatenate([vectors, up_bias.reshape(layers, -1, rows)], axis=1)
    kinds = vectors.shape[1]

    flows = []
    for layer in range(layers):
        first = in_weight[layer][:, : 2 * width]
        second = jnp.concatenate([in_weight[layer][:, 2 * width :], out_weight[layer]], axis=1)
        flows.append(
            (
                Flow(gather_attention(first, second)),
                Flow(gather_up(up_weight[layer])),
                Flow(gather_down(down_weight[layer])),
            )
        )
    attention, up_flow, down_flow = flows[0]
    entering = Flow(to_sequences(inputs))
    vector_flow = Flow(gather_small(vectors.reshape(layers * kinds, rows)))
    cut((), attention, entering, vector_flow)
    cut((), attention, entering, vector_flow)
    residual = entering.result.astype(FULL)
    residual = cut(residual, attention, vector_flow, up_flow)
    residual = cut(residual, attention, vector_flow, up_flow, down_flow)
    residual = drain(residual, vector_flow)
    gathered = vector_flow.result.reshape(-1, layers, kinds, rows).astype(FULL)
    straight = gathered.transpose(1, 2, 0, 3).reshape(layers, kinds, width)
    biases = gathered[:, :, 8:].transpose(1, 0, 2, 3).reshape(layers, kinds - 8, width)
    small = jnp.concatenate([straight[:, :8], biases], axis=1)
    residual = cut(residual, attention)
    leaving = Flow(to_sequences(cotangent))
    records = []
    for layer in range(layers):
        residual = drain(residual, flows[layer][0])
        coming = flows[layer + 1] if layer + 1 < layers else None
        if coming is None:
            residual = cut(residual, leaving)
        residual, record = layer_forward(residual, small[layer], flows[layer], coming, core)
        records.append(record)
    residual = drain(residual, leaving)
    outgoing = Flow(from_sequences(residual))
    upstream = leaving.result.astype(FULL)
    upstream = cut(upstream, outgoing)
    found = [None] * layers
    terms = [None] * layers
    before = ()
    for layer in reversed(range(layers)):
        weights = tuple(flow.result for flow in flows[layer])
        upstream, terms[layer], after = layer_backward(
            upstream, small[layer], weights, records[layer], core, before
        )
        upstream = drain(upstream, *before)
        before = after
        found[layer] = after
    gradient = Flow(from_sequences(upstream))
    drain((), *before, gradient, outgoing)

    sums = lax.psum(jnp.stack(terms), ("dp", "blk", "uly"))
    place = lax.axis_index("dp")
    sliced = lax.dynamic_slice_in_dim(sums, place * rows, rows, 2)
    long = kinds - 8
    up_sums = lax.dynamic_slice_in_dim(
        sums[:, 8:].reshape(layers, -1), place * long * rows, long * rows, 1
    )
    matrices = [[], [], [], []]
    for layer in range(layers):
        attention, up_flow, down_flow = found[layer]
        pairs = attention.result
        whole = [
            jnp.concatenate([pairs[block, 0, kind], pairs[block, 1, kind]], axis=-1)
            for block in range(2)
            for kind in range(2)
        ]
        matrices[0].append(jnp.concatenate(whole[:3], axis=-1))
        matrices[1].append(whole[3])
        matrices[2].append(up_flow.result)
        matrices[3].append(down_flow.result)
    in_sum, out_sum, up_sum, down_sum = (jnp.stack(item).astype(FULL) for item in matrices)
    return (
        outgoing.result,
        gradient.result,
        sliced[:, 0],
        sliced[:, 1],
        in_sum,
        sliced[:, 2],
        sliced[:, 3],
        out_sum,
        sliced[:, 4],
        sliced[:, 5],
        sliced[:, 6],
        up_sum,
        up_sums,
        down_sum,
        sliced[:, 7],
    )


def solution(mesh):
    token = P("dp", ("blk", "uly"), None)
    vector = P(None, "dp")
    matrix = P(None, "dp", None)
    params = (
        vector,
        vector,
        matrix,
        vector,
        vector,
        matrix,
        vector,
        vector,
        vector,
        matrix,
        vector,
        matrix,
        vector,
    )
    specs = (token, token) + params
    return jax.shard_map(shards, mesh=mesh, in_specs=specs, out_specs=specs, check_vma=False)
```

```python
import jax
import jax.numpy as jnp
from jax import lax
from jax.experimental import pallas as pl
from jax.experimental.pallas import tpu as pltpu
from jax.sharding import PartitionSpec as P

HDIM = 64
EPSILON = 1e-05
NEGATIVE = -1e30
LOW = jnp.bfloat16
FULL = jnp.float32
SCALE = HDIM**-0.5
TILE = 256
MIB = 2**20


def dot_nt(left, right):
    return lax.dot_general(left, right, (((1,), (1,)), ((), ())), preferred_element_type=FULL)


def dot_nn(left, right):
    return lax.dot_general(left, right, (((1,), (0,)), ((), ())), preferred_element_type=FULL)


def head_lanes(item, head):
    lane = lax.broadcasted_iota(jnp.int32, item.shape, 1)
    return jnp.where((lane // HDIM) == head, item, jnp.zeros_like(item))


def keep_diagonal(scores):
    keys = lax.broadcasted_iota(jnp.int32, scores.shape, 0)
    rows = lax.broadcasted_iota(jnp.int32, scores.shape, 1)
    return jnp.where(keys <= rows, scores, NEGATIVE)


def join(core, mine, theirs, whole):
    half = mine.shape[0]

    @pl.when(core == 0)
    def _():
        whole[:half] = mine[...]
        whole[half:] = theirs[...]

    @pl.when(core != 0)
    def _():
        whole[:half] = theirs[...]
        whole[half:] = mine[...]


def part(core, whole, mine, theirs):
    half = mine.shape[0]

    @pl.when(core == 0)
    def _():
        mine[...] = whole[:half].astype(mine.dtype)
        theirs[...] = whole[half:].astype(theirs.dtype)

    @pl.when(core != 0)
    def _():
        theirs[...] = whole[:half].astype(theirs.dtype)
        mine[...] = whole[half:].astype(mine.dtype)


def attend_kernel(core_ref, mine_ref, theirs_ref, mixed_mine, mixed_theirs, logsum_ref, qkv, mixed_ref):
    core = core_ref[0]
    for kind in range(3):
        join(core, mine_ref.at[kind, 0], theirs_ref.at[kind, 0], qkv.at[kind])
    length = qkv.shape[1]
    values_t = qkv[2].T
    for start in range(0, length, TILE):
        rows = slice(start, start + TILE)
        queries = qkv[0, rows] * jnp.asarray(SCALE, LOW)
        outs = []
        for head in range(2):
            own = head_lanes(queries, head)
            scores = keep_diagonal(dot_nt(qkv[1, rows], own))
            top = jnp.max(scores, axis=0, keepdims=True)
            if start:
                early = dot_nt(qkv[1, :start], own)
                top = jnp.maximum(top, jnp.max(early, axis=0, keepdims=True))
            raised = jnp.exp(scores - top)
            total = jnp.sum(raised, axis=0, keepdims=True)
            mixed = dot_nn(values_t[:, rows], raised.astype(LOW))
            if start:
                raised = jnp.exp(early - top)
                total = total + jnp.sum(raised, axis=0, keepdims=True)
                mixed = mixed + dot_nn(values_t[:, :start], raised.astype(LOW))
            outs.append((mixed / total)[head * HDIM : (head + 1) * HDIM])
            logsum_ref[0, 0, head : head + 1, rows] = top + jnp.log(total)
        mixed_ref[rows] = jnp.concatenate(outs, axis=0).T.astype(LOW)
    part(core, mixed_ref, mixed_mine.at[0], mixed_theirs.at[0])


def attend(core, mine, theirs):
    three, count, rows, width = mine.shape
    pairs = width // 128
    wide = pl.BlockSpec((3, 1, rows, 128), lambda s, p, core: (0, s, 0, p))
    thin = pl.BlockSpec((1, rows, 128), lambda s, p, core: (s, 0, p))
    return pl.pallas_call(
        attend_kernel,
        grid_spec=pltpu.PrefetchScalarGridSpec(
            num_scalar_prefetch=1,
            grid=(count, pairs),
            in_specs=[wide, wide],
            out_specs=[
                thin,
                thin,
                pl.BlockSpec((1, 1, 8, 2 * rows), lambda s, p, core: (s, p, 0, 0)),
            ],
            scratch_shapes=[pltpu.VMEM((3, 2 * rows, 128), LOW), pltpu.VMEM((2 * rows, 128), LOW)],
        ),
        out_shape=[
            jax.ShapeDtypeStruct((count, rows, width), LOW),
            jax.ShapeDtypeStruct((count, rows, width), LOW),
            jax.ShapeDtypeStruct((count, pairs, 8, 2 * rows), FULL),
        ],
        compiler_params=pltpu.CompilerParams(vmem_limit_bytes=32 * MIB),
        name="attend",
    )(core, mine, theirs)


def attend_back_kernel(
    core_ref,
    mine_ref,
    theirs_ref,
    logsum_ref,
    mixed_mine,
    mixed_theirs,
    slope_mine,
    slope_theirs,
    out_mine,
    out_theirs,
    qkv,
    mixed_ref,
    slope_ref,
    grads,
):
    core = core_ref[0]
    for kind in range(3):
        join(core, mine_ref.at[kind, 0], theirs_ref.at[kind, 0], qkv.at[kind])
    join(core, mixed_mine.at[0], mixed_theirs.at[0], mixed_ref)
    join(core, slope_mine.at[0], slope_theirs.at[0], slope_ref)
    length = qkv.shape[1]
    keys_t = qkv[1].T * jnp.asarray(SCALE, LOW)
    product = (mixed_ref[...].astype(FULL) * slope_ref[...].astype(FULL)).T
    inner = [
        jnp.sum(product[h * HDIM : (h + 1) * HDIM], axis=0, keepdims=True) for h in range(2)
    ]
    for start in range(0, length, TILE):
        rows = slice(start, start + TILE)
        queries = qkv[0, rows] * jnp.asarray(SCALE, LOW)
        slope = slope_ref[rows]
        query_slopes = []
        for head in range(2):
            own = head_lanes(queries, head)
            own_slope = head_lanes(slope, head)
            logsum = logsum_ref[0, 0, head : head + 1, rows]
            query_slope = None
            for first in range(0, start + TILE, TILE):
                span = slice(first, first + TILE)
                scores = dot_nt(qkv[1, span], own)
                if first == start:
                    scores = keep_diagonal(scores)
                shares = jnp.exp(scores - logsum)
                against = dot_nt(qkv[2, span], own_slope)
                slopes = (shares * (against - inner[head][:, rows])).astype(LOW)
                value_slope = dot_nn(shares.astype(LOW), own_slope)
                key_slope = dot_nn(slopes, own)
                if first == start and head == 0:
                    grads[2, span] = value_slope
                    grads[1, span] = key_slope
                else:
                    grads[2, span] += value_slope
                    grads[1, span] += key_slope
                piece = dot_nn(keys_t[:, span], slopes)
                query_slope = piece if query_slope is None else query_slope + piece
            query_slopes.append(query_slope[head * HDIM : (head + 1) * HDIM])
        grads[0, rows] = jnp.concatenate(query_slopes, axis=0).T
    for kind in range(3):
        part(core, grads.at[kind], out_mine.at[kind, 0], out_theirs.at[kind, 0])


def attend_back(core, mine, theirs, logsum, mixed, slope):
    three, count, rows, width = mine.shape
    pairs = width // 128
    wide = pl.BlockSpec((3, 1, rows, 128), lambda s, p, core: (0, s, 0, p))
    thin = pl.BlockSpec((1, rows, 128), lambda s, p, core: (s, 0, p))
    sums = pl.BlockSpec((1, 1, 8, 2 * rows), lambda s, p, core: (s, p, 0, 0))
    return pl.pallas_call(
        attend_back_kernel,
        grid_spec=pltpu.PrefetchScalarGridSpec(
            num_scalar_prefetch=1,
            grid=(count, pairs),
            in_specs=[wide, wide, sums, thin, thin, thin, thin],
            out_specs=[wide, wide],
            scratch_shapes=[
                pltpu.VMEM((3, 2 * rows, 128), LOW),
                pltpu.VMEM((2 * rows, 128), LOW),
                pltpu.VMEM((2 * rows, 128), LOW),
                pltpu.VMEM((3, 2 * rows, 128), FULL),
            ],
        ),
        out_shape=[jax.ShapeDtypeStruct(mine.shape, LOW)] * 2,
        compiler_params=pltpu.CompilerParams(vmem_limit_bytes=32 * MIB),
        name="attend_back",
    )(core, mine, theirs, logsum, *mixed, *slope)


def normalize(residual, gain, shift):
    average = jnp.mean(residual, axis=-1, keepdims=True)
    centred = residual - average
    variance = jnp.mean(centred * centred, axis=-1, keepdims=True)
    return centred * lax.rsqrt(variance + EPSILON) * gain + shift


def norm_backward(residual, gain, slope):
    average = jnp.mean(residual, axis=-1, keepdims=True)
    centred = residual - average
    scale = lax.rsqrt(jnp.mean(centred * centred, axis=-1, keepdims=True) + EPSILON)
    unit = centred * scale
    raised = slope * gain
    along = jnp.mean(raised * unit, axis=-1, keepdims=True)
    level = jnp.mean(raised, axis=-1, keepdims=True)
    return scale * (raised - level - unit * along), token_sum(slope * unit), token_sum(slope)


def sum_small(held):
    arrived = yield [(held, "blk", 1)]
    held = held + arrived[0]
    arrived = yield [(held, "uly", 1)]
    held = held + arrived[0]
    for mask in masks_of("dp"):
        arrived = yield [(held, "dp", mask)]
        held = held + arrived[0]
    return held


def gelu(hidden):
    return jax.nn.gelu(hidden, approximate=True)


def matmul(left, right):
    return jnp.dot(left, right, preferred_element_type=FULL)


def contract(left, right):
    return jnp.einsum("std,ste->de", left, right, preferred_element_type=FULL).astype(LOW)


def transposed(left, right):
    return jnp.einsum("ste,de->std", left, right, preferred_element_type=FULL)


def swap(item, axis, mask=1):
    count = lax.axis_size(axis)
    return lax.ppermute(item, axis, [(i, i ^ mask) for i in range(count)])


def bit_of(axis, mask=1):
    return (lax.axis_index(axis) & mask) != 0


def masks_of(axis):
    count = lax.axis_size(axis)
    masks = []
    mask = 1
    while mask < count:
        masks.append(mask)
        mask *= 2
    return masks


def ordered(own, other, bit, axis):
    low = jnp.where(bit, other, own)
    high = jnp.where(bit, own, other)
    return jnp.stack([low, high], axis=axis)


def side_by_side(own, other, bit):
    low = jnp.where(bit, other, own)
    high = jnp.where(bit, own, other)
    return jnp.concatenate([low, high], axis=-1)


def chosen(item, bit, axis):
    return lax.dynamic_index_in_dim(item, bit.astype(jnp.int32), axis, keepdims=False)


def added(left, right):
    return (left.astype(FULL) + right.astype(FULL)).astype(LOW)


class Flow:
    def __init__(self, steps):
        self.steps = steps
        self.result = None
        self.done = False
        self.flying = None
        self.waiting = None
        self.advance(None)

    def advance(self, arrived):
        try:
            self.waiting = self.steps.send(arrived)
        except StopIteration as stop:
            self.done = True
            self.waiting = None
            self.result = stop.value

    def launch(self):
        if not self.done:
            self.flying = [swap(*send) for send in self.waiting]
            self.waiting = None


def cut(live, *flows):
    flows = [flow for flow in flows if not flow.done]
    sends = [
        flow.flying if flow.flying is not None else [item[0] for item in flow.waiting]
        for flow in flows
    ]
    live, sends = lax.optimization_barrier((live, sends))
    for flow, arrays in zip(flows, sends):
        if flow.flying is not None:
            flow.flying = None
            flow.advance(arrays)
        else:
            flow.waiting = [(a,) + item[1:] for a, item in zip(arrays, flow.waiting)]
        flow.launch()
    return live


def drain(live, *flows):
    while not all(flow.done for flow in flows):
        live = cut(live, *flows)
    return live


def grown(held, other, mask, flip=None):
    bit = bit_of("dp", mask)
    if flip is not None:
        bit = bit ^ flip
    joined = ordered(held, other, bit, -3)
    return joined.reshape(held.shape[:-3] + (-1,) + held.shape[-2:])


def gather_small(piece):
    held = piece[None]
    for mask in reversed(masks_of("dp")):
        (other,) = yield [(held, "dp", mask)]
        held = grown(held, other, mask)
    return held


def rows_of(held):
    return held.reshape(held.shape[:-3] + (-1, held.shape[-1]))


def quarter_of(block):
    width = block.shape[1] // 4
    start = (2 * lax.axis_index("uly") + lax.axis_index("blk")) * width
    return lax.dynamic_slice_in_dim(block, start, width, 1)


def gather_attention(first, second):
    held = jnp.stack([quarter_of(first), quarter_of(second)])[:, None]
    masks = masks_of("dp")
    for mask in reversed(masks[1:]):
        (other,) = yield [(held, "dp", mask)]
        held = grown(held, other, mask)
    left, right = held[0], held[1]
    place = bit_of("uly")
    other_left, other_right = yield [(left, "dp", masks[0]), (right, "uly", 1)]
    left = grown(left, other_left, masks[0])
    right = ordered(right, other_right, place, 0)
    other_left, other_right = yield [(left, "uly", 1), (right, "dp", masks[0])]
    left = rows_of(ordered(left, other_left, place, 0))
    right = rows_of(grown(right, other_right, masks[0]))
    other = yield [(left, "blk", 1), (right, "blk", 1)]
    return (left, right), tuple(other)


def gather_up(block):
    width = block.shape[1] // 4
    start = (2 * lax.axis_index("blk") + lax.axis_index("uly")) * width
    held = lax.dynamic_slice_in_dim(block, start, width, 1)[None]
    for mask in reversed(masks_of("dp")):
        (other,) = yield [(held, "dp", mask)]
        held = grown(held, other, mask)
    rows = rows_of(held)
    (other,) = yield [(rows, "uly", 1)]
    own = ordered(rows, other, bit_of("uly"), 0)
    (other,) = yield [(own, "blk", 1)]
    return own, other


def gather_down(block):
    width = block.shape[1] // 2
    held = lax.dynamic_slice_in_dim(block, lax.axis_index("blk") * width, width, 1)[None]
    masks = masks_of("dp")
    for mask in reversed(masks):
        (other,) = yield [(held, "dp", mask)]
        held = grown(held, other, mask, bit_of("blk") if mask == masks[-1] else None)
    own = held.reshape(2, -1, width)
    (other,) = yield [(own, "blk", 1)]
    return own, other


def halved(held, bit):
    return chosen(held, bit, -3), chosen(held, ~bit, -3)


def split_rows(held):
    return held.reshape(held.shape[:-3] + (-1, 2) + held.shape[-2:])


def reduce_attention(own, other):
    count = lax.axis_size("dp")
    masks = masks_of("dp")
    place = bit_of("uly")
    arrived = yield [(other[0], "blk", 1), (other[1], "blk", 1)]
    left, right = added(own[0], arrived[0]), added(own[1], arrived[1])
    two, rows, width = left.shape
    left = left.reshape(2, count, rows // count, width)
    right = right.reshape(2, count, rows // count, width)
    keep_left, send_left = chosen(left, place, 0), chosen(left, ~place, 0)
    bit = bit_of("dp", masks[0])
    keep_right, send_right = halved(split_rows(right), bit)
    arrived = yield [(send_left, "uly", 1), (send_right, "dp", masks[0])]
    left, right = added(keep_left, arrived[0]), added(keep_right, arrived[1])
    keep_left, send_left = halved(split_rows(left), bit)
    keep_right, send_right = chosen(right, place, 0), chosen(right, ~place, 0)
    arrived = yield [(send_left, "dp", masks[0]), (send_right, "uly", 1)]
    held = jnp.stack([added(keep_left, arrived[0]), added(keep_right, arrived[1])])
    for mask in masks[1:]:
        keep, send = halved(split_rows(held), bit_of("dp", mask))
        (other,) = yield [(send, "dp", mask)]
        held = added(keep, other)
    held = held[:, 0]
    (other,) = yield [(held, "uly", 1)]
    held = ordered(held, other, place, 1)
    (other,) = yield [(held, "blk", 1)]
    return ordered(held, other, bit_of("blk"), 1)


def reduce_up(own, other):
    count = lax.axis_size("dp")
    place = bit_of("uly")
    (arrived,) = yield [(other, "blk", 1)]
    held = added(own, arrived)
    two, rows, width = held.shape
    keep, send = chosen(held, place, 0), chosen(held, ~place, 0)
    (arrived,) = yield [(send, "uly", 1)]
    held = added(keep, arrived).reshape(count, rows // count, width)
    for mask in masks_of("dp"):
        keep, send = halved(split_rows(held), bit_of("dp", mask))
        (arrived,) = yield [(send, "dp", mask)]
        held = added(keep, arrived)
    held = held[0]
    (arrived,) = yield [(held, "uly", 1)]
    held = ordered(held, arrived, place, 0)
    (arrived,) = yield [(held, "blk", 1)]
    every = ordered(held, arrived, bit_of("blk"), 0)
    return jnp.concatenate([every[i, j] for i in range(2) for j in range(2)], axis=-1)


def reduce_down(own, other):
    count = lax.axis_size("dp")
    masks = masks_of("dp")
    (arrived,) = yield [(other, "blk", 1)]
    held = added(own, jnp.stack([arrived[1], arrived[0]]))
    width = held.shape[2]
    held = held.reshape(count, -1, width)
    for mask in masks:
        bit = bit_of("dp", mask)
        if mask == masks[-1]:
            bit = bit ^ bit_of("blk")
        keep, send = halved(split_rows(held), bit)
        (arrived,) = yield [(send, "dp", mask)]
        held = added(keep, arrived)
    held = held[0]
    (arrived,) = yield [(held, "uly", 1)]
    held = added(held, arrived)
    (arrived,) = yield [(held, "blk", 1)]
    return side_by_side(held, arrived, bit_of("blk"))


def to_sequences(local):
    place = bit_of("uly")
    count, rows, width = local.shape
    paired = local.reshape(2, count // 2, rows, width)
    (arrived,) = yield [(chosen(paired, ~place, 0), "uly", 1)]
    joined = ordered(chosen(paired, place, 0), arrived, place, 1)
    return joined.reshape(count // 2, 2 * rows, width)


def from_sequences(held):
    place = bit_of("uly")
    count, rows, width = held.shape
    paired = held.reshape(count, 2, rows // 2, width)
    (arrived,) = yield [(chosen(paired, ~place, 1).astype(LOW), "uly", 1)]
    joined = ordered(chosen(paired, place, 1), arrived.astype(FULL), place, 0)
    return joined.reshape(2 * count, rows // 2, width)


def token_sum(item):
    return jnp.sum(item.astype(FULL), axis=(0, 1))[None]


def halves_of(item):
    half = item.shape[-1] // 2
    low, high = item[..., :half], item[..., half:]
    bit = bit_of("blk")
    return jnp.where(bit, high, low), jnp.where(bit, low, high)


def layer_forward(residual, small, flows, coming, core):
    attention, up_flow, down_flow = flows
    first_gain, first_shift, query_bias, value_bias, out_bias = (small[i : i + 1] for i in range(5))
    second_gain, second_shift, down_bias = (small[i : i + 1] for i in range(5, 8))
    bit = bit_of("blk")
    next_attention, next_up, next_down = coming if coming else (None, None, None)

    def with_next(*items):
        return [item for item in items if item is not None]

    own, other = attention.result
    normed = normalize(residual, first_gain, first_shift).astype(LOW)
    normed = cut(normed, up_flow, down_flow, *with_next(next_attention))
    query_biases, value_biases = halves_of(query_bias), halves_of(value_bias)

    def project(weights, i):
        (query, key), (value, unused) = weights
        return jnp.stack(
            [
                (matmul(normed, query) + query_biases[i]).astype(LOW),
                matmul(normed, key).astype(LOW),
                (matmul(normed, value) + value_biases[i]).astype(LOW),
            ]
        )

    away = swap(project(other, 1), "blk")
    mine = project(own, 0)
    mine, away = cut((mine, away), *([next_attention] if coming else [down_flow]))
    mixed_mine, mixed_theirs, logsum = attend(core, mine, away)
    mixed_mine, mixed_theirs = cut(
        (mixed_mine, mixed_theirs),
        up_flow,
        *([down_flow, next_attention, next_up] if coming else []),
    )
    arrived = swap(mixed_theirs, "blk")
    mixed = side_by_side(mixed_mine, arrived, bit)
    columns = side_by_side(matmul(mixed, own[1][1]), matmul(mixed, other[1][1]), bit)
    middle = residual + columns + out_bias
    normed_two = normalize(middle, second_gain, second_shift).astype(LOW)
    middle, normed_two = cut(
        (middle, normed_two), up_flow, down_flow, *with_next(next_attention, next_up)
    )
    middle, normed_two = drain((middle, normed_two), up_flow)
    low_biases, high_biases = small[8:10], small[10:12]
    up_biases = jnp.where(bit, high_biases, low_biases), jnp.where(bit, low_biases, high_biases)
    hidden = []
    active = []
    for weights, bias in zip(up_flow.result, up_biases):
        parts = [
            matmul(normed_two, weights[i]) + bias[i : i + 1] for i in range(2)
        ]
        hidden.append(parts)
        active.append(jnp.concatenate([gelu(item).astype(LOW) for item in parts], axis=-1))
    active, middle = cut(
        (active, middle), down_flow, *with_next(next_attention, next_up, next_down)
    )
    active, middle = drain((active, middle), down_flow)
    down_own, down_other = down_flow.result
    left = matmul(active[0], down_own[0]) + matmul(active[1], down_own[1])
    right = matmul(active[0], down_other[1]) + matmul(active[1], down_other[0])
    result = middle + side_by_side(left, right, bit) + down_bias
    if coming:
        result = cut(result, next_attention)
    record = (residual, normed, mine, away, logsum, mixed_mine, mixed_theirs, mixed)
    return result, record + (middle, normed_two, hidden, active)


def layer_backward(upstream, small, weights, record, core, before):
    (own, other), (up_own, up_other), (down_own, down_other) = weights
    first_gain, second_gain = small[0:1], small[5:6]
    residual, normed, mine, away, logsum, mixed_mine, mixed_theirs, mixed = record[:8]
    middle, normed_two, hidden, active = record[8:]
    bit = bit_of("blk")

    down_bias_slope = token_sum(upstream)
    low_own, low_other = halves_of(upstream.astype(LOW))
    down_slopes = [
        jnp.stack([contract(active[i], low_other) for i in range(2)]),
        jnp.stack([contract(active[i], low_own) for i in range(2)]),
    ]
    down_flow = Flow(reduce_down(down_slopes[1], down_slopes[0]))
    low_own, low_other, upstream = cut((low_own, low_other, upstream), down_flow, *before)
    active_slopes = [
        transposed(low_own, down_own[0]) + transposed(low_other, down_other[1]),
        transposed(low_own, down_own[1]) + transposed(low_other, down_other[0]),
    ]
    low_hidden = []
    bias_slopes = []
    for slope, parts in zip(active_slopes, hidden):
        width = parts[0].shape[-1]
        for i, item in enumerate(parts):
            unused, pullback = jax.vjp(gelu, item)
            hidden_slope = pullback(slope[..., i * width : (i + 1) * width])[0]
            bias_slopes.append(token_sum(hidden_slope))
            low_hidden.append(hidden_slope.astype(LOW))
    low_hidden = cut(low_hidden, down_flow, *before)
    low_biases = [jnp.where(bit, bias_slopes[2 + i], bias_slopes[i]) for i in range(2)]
    high_biases = [jnp.where(bit, bias_slopes[i], bias_slopes[2 + i]) for i in range(2)]
    up_slopes = [
        jnp.stack([contract(normed_two, low_hidden[2 + i]) for i in range(2)]),
        jnp.stack([contract(normed_two, low_hidden[i]) for i in range(2)]),
    ]
    up_flow = Flow(reduce_up(up_slopes[1], up_slopes[0]))
    low_hidden = cut(low_hidden, up_flow)
    norm_slope = (
        transposed(low_hidden[0], up_own[0])
        + transposed(low_hidden[1], up_own[1])
        + transposed(low_hidden[2], up_other[0])
        + transposed(low_hidden[3], up_other[1])
    )
    through, second_gain_slope, second_shift_slope = norm_backward(middle, second_gain, norm_slope)
    middle_slope = upstream + through
    middle_slope = cut(middle_slope, up_flow, *before)

    out_bias_slope = token_sum(middle_slope)
    low_own, low_other = halves_of(middle_slope.astype(LOW))
    mixed_slope = transposed(low_own, own[1][1]) + transposed(low_other, other[1][1])
    slope_own, slope_other = halves_of(mixed_slope.astype(LOW))
    slope_away = swap(slope_other, "blk")
    out_slopes = contract(mixed, low_own), contract(mixed, low_other)
    slope_own, slope_away, out_slopes = cut((slope_own, slope_away, out_slopes), *before)
    grads_mine, grads_theirs = attend_back(
        core, mine, away, logsum, (mixed_mine, mixed_theirs), (slope_own, slope_away)
    )
    grads_mine, grads_theirs, middle_slope = cut(
        (grads_mine, grads_theirs, middle_slope), down_flow, up_flow, *before
    )
    grads_away = swap(grads_theirs, "blk")
    first, second = [], []
    for grads, out_slope in zip((grads_mine, grads_away), out_slopes):
        slopes = [contract(normed, grads[i]) for i in range(3)]
        first.append(jnp.stack(slopes[:2]))
        second.append(jnp.stack([slopes[2], out_slope]))
    attention_flow = Flow(reduce_attention((first[0], second[0]), (first[1], second[1])))
    grads_mine, grads_away, middle_slope = cut(
        (grads_mine, grads_away, middle_slope), attention_flow, *before
    )
    query_bias_slope = side_by_side(token_sum(grads_mine[0]), token_sum(grads_away[0]), bit)
    value_bias_slope = side_by_side(token_sum(grads_mine[2]), token_sum(grads_away[2]), bit)
    first_slope = 0.0
    for grads, (pair, last) in ((grads_mine, own), (grads_away, other)):
        first_slope = (
            first_slope
            + transposed(grads[0], pair[0])
            + transposed(grads[1], pair[1])
            + transposed(grads[2], last[0])
        )
    through, first_gain_slope, first_shift_slope = norm_backward(residual, first_gain, first_slope)
    upstream = middle_slope + through
    upstream = cut(upstream, attention_flow, up_flow, down_flow, *before)
    vectors = [
        first_gain_slope,
        first_shift_slope,
        query_bias_slope,
        value_bias_slope,
        out_bias_slope,
        second_gain_slope,
        second_shift_slope,
        down_bias_slope,
    ]
    terms = jnp.concatenate(vectors + low_biases + high_biases)
    return upstream, terms, (attention_flow, up_flow, down_flow)


def shards(
    inputs,
    cotangent,
    first_gain,
    first_shift,
    in_weight,
    query_bias,
    value_bias,
    out_weight,
    out_bias,
    second_gain,
    second_shift,
    up_weight,
    up_bias,
    down_weight,
    down_bias,
):
    layers, rows = in_weight.shape[0], in_weight.shape[1]
    width = out_weight.shape[2]
    core = lax.axis_index("blk").astype(jnp.int32).reshape(1)
    vectors = jnp.stack(
        [
            first_gain,
            first_shift,
            query_bias,
            value_bias,
            out_bias,
            second_gain,
            second_shift,
            down_bias,
        ],
        axis=1,
    )
    vectors = jnp.concatenate([vectors, up_bias.reshape(layers, -1, rows)], axis=1)
    kinds = vectors.shape[1]

    flows = []
    for layer in range(layers):
        first = in_weight[layer][:, : 2 * width]
        second = jnp.concatenate([in_weight[layer][:, 2 * width :], out_weight[layer]], axis=1)
        flows.append(
            (
                Flow(gather_attention(first, second)),
                Flow(gather_up(up_weight[layer])),
                Flow(gather_down(down_weight[layer])),
            )
        )
    attention, up_flow, down_flow = flows[0]
    entering = Flow(to_sequences(inputs))
    vector_flow = Flow(gather_small(vectors.reshape(layers * kinds, rows)))
    cut((), attention, entering, vector_flow)
    cut((), attention, entering, vector_flow)
    residual = entering.result.astype(FULL)
    residual = cut(residual, attention, vector_flow, up_flow)
    residual = cut(residual, attention, vector_flow, up_flow, down_flow)
    residual = drain(residual, vector_flow)
    gathered = vector_flow.result.reshape(-1, layers, kinds, rows).astype(FULL)
    straight = gathered.transpose(1, 2, 0, 3).reshape(layers, kinds, width)
    biases = gathered[:, :, 8:].transpose(1, 0, 2, 3).reshape(layers, kinds - 8, width)
    small = jnp.concatenate([straight[:, :8], biases], axis=1)
    residual = cut(residual, attention, up_flow, down_flow)
    leaving = Flow(to_sequences(cotangent))
    records = []
    for layer in range(layers):
        residual = drain(residual, flows[layer][0])
        coming = flows[layer + 1] if layer + 1 < layers else None
        if coming is None:
            residual = cut(residual, leaving)
        residual, record = layer_forward(residual, small[layer], flows[layer], coming, core)
        records.append(record)
    residual = drain(residual, leaving)
    outgoing = Flow(from_sequences(residual))
    upstream = leaving.result.astype(FULL)
    upstream = cut(upstream, outgoing)
    found = [None] * layers
    terms = [None] * layers
    before = ()
    for layer in reversed(range(layers)):
        weights = tuple(flow.result for flow in flows[layer])
        upstream, terms[layer], after = layer_backward(
            upstream, small[layer], weights, records[layer], core, before
        )
        upstream = drain(upstream, *before)
        before = after
        found[layer] = after
    gradient = Flow(from_sequences(upstream))
    totals = Flow(sum_small(jnp.concatenate(terms)))
    drain((), *before, gradient, totals, outgoing)

    sums = totals.result.reshape(layers, kinds, width)
    place = lax.axis_index("dp")
    sliced = lax.dynamic_slice_in_dim(sums, place * rows, rows, 2)
    long = kinds - 8
    up_sums = lax.dynamic_slice_in_dim(
        sums[:, 8:].reshape(layers, -1), place * long * rows, long * rows, 1
    )
    matrices = [[], [], [], []]
    for layer in range(layers):
        attention, up_flow, down_flow = found[layer]
        pairs = attention.result
        whole = [
            jnp.concatenate([pairs[block, 0, kind], pairs[block, 1, kind]], axis=-1)
            for block in range(2)
            for kind in range(2)
        ]
        matrices[0].append(jnp.concatenate(whole[:3], axis=-1))
        matrices[1].append(whole[3])
        matrices[2].append(up_flow.result)
        matrices[3].append(down_flow.result)
    in_sum, out_sum, up_sum, down_sum = (jnp.stack(item).astype(FULL) for item in matrices)
    return (
        outgoing.result,
        gradient.result,
        sliced[:, 0],
        sliced[:, 1],
        in_sum,
        sliced[:, 2],
        sliced[:, 3],
        out_sum,
        sliced[:, 4],
        sliced[:, 5],
        sliced[:, 6],
        up_sum,
        up_sums,
        down_sum,
        sliced[:, 7],
    )


def solution(mesh):
    token = P("dp", ("blk", "uly"), None)
    vector = P(None, "dp")
    matrix = P(None, "dp", None)
    params = (
        vector,
        vector,
        matrix,
        vector,
        vector,
        matrix,
        vector,
        vector,
        vector,
        matrix,
        vector,
        matrix,
        vector,
    )
    specs = (token, token) + params
    return jax.shard_map(shards, mesh=mesh, in_specs=specs, out_specs=specs, check_vma=False)
```

```python
import jax
import jax.numpy as jnp
from jax import lax
from jax.experimental import pallas as pl
from jax.experimental.pallas import tpu as pltpu
from jax.sharding import PartitionSpec as P

HDIM = 64
EPSILON = 1e-05
NEGATIVE = -1e30
LOW = jnp.bfloat16
FULL = jnp.float32
SCALE = HDIM**-0.5
TILE = 256
MIB = 2**20


def dot_nt(left, right):
    return lax.dot_general(left, right, (((1,), (1,)), ((), ())), preferred_element_type=FULL)


def dot_nn(left, right):
    return lax.dot_general(left, right, (((1,), (0,)), ((), ())), preferred_element_type=FULL)


def head_lanes(item, head):
    lane = lax.broadcasted_iota(jnp.int32, item.shape, 1)
    return jnp.where((lane // HDIM) == head, item, jnp.zeros_like(item))


def keep_diagonal(scores):
    keys = lax.broadcasted_iota(jnp.int32, scores.shape, 0)
    rows = lax.broadcasted_iota(jnp.int32, scores.shape, 1)
    return jnp.where(keys <= rows, scores, NEGATIVE)


def join(core, mine, theirs, whole):
    half = mine.shape[0]

    @pl.when(core == 0)
    def _():
        whole[:half] = mine[...]
        whole[half:] = theirs[...]

    @pl.when(core != 0)
    def _():
        whole[:half] = theirs[...]
        whole[half:] = mine[...]


def part(core, whole, mine, theirs):
    half = mine.shape[0]

    @pl.when(core == 0)
    def _():
        mine[...] = whole[:half].astype(mine.dtype)
        theirs[...] = whole[half:].astype(theirs.dtype)

    @pl.when(core != 0)
    def _():
        theirs[...] = whole[:half].astype(theirs.dtype)
        mine[...] = whole[half:].astype(mine.dtype)


def attend_kernel(core_ref, mine_ref, theirs_ref, mixed_mine, mixed_theirs, logsum_ref, qkv, mixed_ref):
    core = core_ref[0]
    for kind in range(3):
        join(core, mine_ref.at[kind, 0], theirs_ref.at[kind, 0], qkv.at[kind])
    length = qkv.shape[1]
    values_t = qkv[2].T
    for start in range(0, length, TILE):
        rows = slice(start, start + TILE)
        queries = qkv[0, rows] * jnp.asarray(SCALE, LOW)
        outs = []
        for head in range(2):
            own = head_lanes(queries, head)
            scores = keep_diagonal(dot_nt(qkv[1, rows], own))
            top = jnp.max(scores, axis=0, keepdims=True)
            if start:
                early = dot_nt(qkv[1, :start], own)
                top = jnp.maximum(top, jnp.max(early, axis=0, keepdims=True))
            raised = jnp.exp(scores - top)
            total = jnp.sum(raised, axis=0, keepdims=True)
            mixed = dot_nn(values_t[:, rows], raised.astype(LOW))
            if start:
                raised = jnp.exp(early - top)
                total = total + jnp.sum(raised, axis=0, keepdims=True)
                mixed = mixed + dot_nn(values_t[:, :start], raised.astype(LOW))
            outs.append((mixed / total)[head * HDIM : (head + 1) * HDIM])
            logsum_ref[0, 0, head : head + 1, rows] = top + jnp.log(total)
        mixed_ref[rows] = jnp.concatenate(outs, axis=0).T.astype(LOW)
    part(core, mixed_ref, mixed_mine.at[0], mixed_theirs.at[0])


def attend(core, mine, theirs):
    three, count, rows, width = mine.shape
    pairs = width // 128
    wide = pl.BlockSpec((3, 1, rows, 128), lambda s, p, core: (0, s, 0, p))
    thin = pl.BlockSpec((1, rows, 128), lambda s, p, core: (s, 0, p))
    return pl.pallas_call(
        attend_kernel,
        grid_spec=pltpu.PrefetchScalarGridSpec(
            num_scalar_prefetch=1,
            grid=(count, pairs),
            in_specs=[wide, wide],
            out_specs=[
                thin,
                thin,
                pl.BlockSpec((1, 1, 8, 2 * rows), lambda s, p, core: (s, p, 0, 0)),
            ],
            scratch_shapes=[pltpu.VMEM((3, 2 * rows, 128), LOW), pltpu.VMEM((2 * rows, 128), LOW)],
        ),
        out_shape=[
            jax.ShapeDtypeStruct((count, rows, width), LOW),
            jax.ShapeDtypeStruct((count, rows, width), LOW),
            jax.ShapeDtypeStruct((count, pairs, 8, 2 * rows), FULL),
        ],
        compiler_params=pltpu.CompilerParams(vmem_limit_bytes=32 * MIB),
        name="attend",
    )(core, mine, theirs)


def attend_back_kernel(
    core_ref,
    mine_ref,
    theirs_ref,
    logsum_ref,
    mixed_mine,
    mixed_theirs,
    slope_mine,
    slope_theirs,
    out_mine,
    out_theirs,
    qkv,
    mixed_ref,
    slope_ref,
    grads,
):
    core = core_ref[0]
    for kind in range(3):
        join(core, mine_ref.at[kind, 0], theirs_ref.at[kind, 0], qkv.at[kind])
    join(core, mixed_mine.at[0], mixed_theirs.at[0], mixed_ref)
    join(core, slope_mine.at[0], slope_theirs.at[0], slope_ref)
    length = qkv.shape[1]
    keys_t = qkv[1].T * jnp.asarray(SCALE, LOW)
    product = (mixed_ref[...].astype(FULL) * slope_ref[...].astype(FULL)).T
    inner = [
        jnp.sum(product[h * HDIM : (h + 1) * HDIM], axis=0, keepdims=True) for h in range(2)
    ]
    for start in range(0, length, TILE):
        rows = slice(start, start + TILE)
        queries = qkv[0, rows] * jnp.asarray(SCALE, LOW)
        slope = slope_ref[rows]
        query_slopes = []
        for head in range(2):
            own = head_lanes(queries, head)
            own_slope = head_lanes(slope, head)
            logsum = logsum_ref[0, 0, head : head + 1, rows]
            query_slope = None
            for first in range(0, start + TILE, TILE):
                span = slice(first, first + TILE)
                scores = dot_nt(qkv[1, span], own)
                if first == start:
                    scores = keep_diagonal(scores)
                shares = jnp.exp(scores - logsum)
                against = dot_nt(qkv[2, span], own_slope)
                slopes = (shares * (against - inner[head][:, rows])).astype(LOW)
                value_slope = dot_nn(shares.astype(LOW), own_slope)
                key_slope = dot_nn(slopes, own)
                if first == start and head == 0:
                    grads[2, span] = value_slope
                    grads[1, span] = key_slope
                else:
                    grads[2, span] += value_slope
                    grads[1, span] += key_slope
                piece = dot_nn(keys_t[:, span], slopes)
                query_slope = piece if query_slope is None else query_slope + piece
            query_slopes.append(query_slope[head * HDIM : (head + 1) * HDIM])
        grads[0, rows] = jnp.concatenate(query_slopes, axis=0).T
    for kind in range(3):
        part(core, grads.at[kind], out_mine.at[kind, 0], out_theirs.at[kind, 0])


def attend_back(core, mine, theirs, logsum, mixed, slope):
    three, count, rows, width = mine.shape
    pairs = width // 128
    wide = pl.BlockSpec((3, 1, rows, 128), lambda s, p, core: (0, s, 0, p))
    thin = pl.BlockSpec((1, rows, 128), lambda s, p, core: (s, 0, p))
    sums = pl.BlockSpec((1, 1, 8, 2 * rows), lambda s, p, core: (s, p, 0, 0))
    return pl.pallas_call(
        attend_back_kernel,
        grid_spec=pltpu.PrefetchScalarGridSpec(
            num_scalar_prefetch=1,
            grid=(count, pairs),
            in_specs=[wide, wide, sums, thin, thin, thin, thin],
            out_specs=[wide, wide],
            scratch_shapes=[
                pltpu.VMEM((3, 2 * rows, 128), LOW),
                pltpu.VMEM((2 * rows, 128), LOW),
                pltpu.VMEM((2 * rows, 128), LOW),
                pltpu.VMEM((3, 2 * rows, 128), FULL),
            ],
        ),
        out_shape=[jax.ShapeDtypeStruct(mine.shape, LOW)] * 2,
        compiler_params=pltpu.CompilerParams(vmem_limit_bytes=32 * MIB),
        name="attend_back",
    )(core, mine, theirs, logsum, *mixed, *slope)


def normalize(residual, gain, shift):
    average = jnp.mean(residual, axis=-1, keepdims=True)
    centred = residual - average
    variance = jnp.mean(centred * centred, axis=-1, keepdims=True)
    return centred * lax.rsqrt(variance + EPSILON) * gain + shift


def norm_backward(residual, gain, slope):
    average = jnp.mean(residual, axis=-1, keepdims=True)
    centred = residual - average
    scale = lax.rsqrt(jnp.mean(centred * centred, axis=-1, keepdims=True) + EPSILON)
    unit = centred * scale
    raised = slope * gain
    along = jnp.mean(raised * unit, axis=-1, keepdims=True)
    level = jnp.mean(raised, axis=-1, keepdims=True)
    return scale * (raised - level - unit * along), token_sum(slope * unit), token_sum(slope)


def partners(item):
    return [(item, "uly", 1), (item, "blk", 1), (item, ("blk", "uly"), 3)]


def far_sends(items):
    near = masks_of("dp")[-2]
    return [(item, "dp", (i + 1) * near) for i, item in enumerate(items)]


def sum_small(held):
    arrived = yield partners(held)
    held = total(held, *arrived)
    for mask in masks_of("dp")[:-2]:
        arrived = yield [(held, "dp", mask)]
        held = total(held, *arrived)
    arrived = yield far_sends([held] * 3)
    return total(held, *arrived)


def gather_far(held):
    near, far = masks_of("dp")[-2:]
    first, second, both = yield far_sends([held] * 3)
    low = ordered(held, first, bit_of("dp", near), -3)
    high = ordered(second, both, bit_of("dp", near), -3)
    joined = ordered(low, high, bit_of("dp", far), -5)
    return joined.reshape(held.shape[:-3] + (4,) + held.shape[-2:])


def reduce_far(held):
    place = lax.axis_index("dp") // masks_of("dp")[-2]
    axis = held.ndim - 3
    parts = [lax.dynamic_index_in_dim(held, place ^ i, axis, keepdims=False) for i in range(4)]
    arrived = yield far_sends(parts[1:])
    return total(parts[0], *arrived)


def gather_partners(held):
    along, across, both = yield partners(held)
    place = bit_of("uly")
    return ordered(ordered(held, along, place, 0), ordered(across, both, place, 0), bit_of("blk"), 0)


def gelu(hidden):
    return jax.nn.gelu(hidden, approximate=True)


def matmul(left, right):
    return jnp.dot(left, right, preferred_element_type=FULL)


def contract(left, right):
    return jnp.einsum("std,ste->de", left, right, preferred_element_type=FULL).astype(LOW)


def transposed(left, right):
    return jnp.einsum("ste,de->std", left, right, preferred_element_type=FULL)


def swap(item, axis, mask=1):
    count = 4 if isinstance(axis, tuple) else lax.axis_size(axis)
    return lax.ppermute(item, axis, [(i, i ^ mask) for i in range(count)])


def bit_of(axis, mask=1):
    return (lax.axis_index(axis) & mask) != 0


def masks_of(axis):
    count = lax.axis_size(axis)
    masks = []
    mask = 1
    while mask < count:
        masks.append(mask)
        mask *= 2
    return masks


def ordered(own, other, bit, axis):
    low = jnp.where(bit, other, own)
    high = jnp.where(bit, own, other)
    return jnp.stack([low, high], axis=axis)


def side_by_side(own, other, bit):
    low = jnp.where(bit, other, own)
    high = jnp.where(bit, own, other)
    return jnp.concatenate([low, high], axis=-1)


def chosen(item, bit, axis):
    return lax.dynamic_index_in_dim(item, bit.astype(jnp.int32), axis, keepdims=False)


def total(*items):
    return sum(item.astype(FULL) for item in items).astype(items[0].dtype)


def added(left, right):
    return (left.astype(FULL) + right.astype(FULL)).astype(LOW)


class Flow:
    def __init__(self, steps):
        self.steps = steps
        self.result = None
        self.done = False
        self.flying = None
        self.waiting = None
        self.advance(None)

    def advance(self, arrived):
        try:
            self.waiting = self.steps.send(arrived)
        except StopIteration as stop:
            self.done = True
            self.waiting = None
            self.result = stop.value

    def launch(self):
        if not self.done:
            self.flying = [swap(*send) for send in self.waiting]
            self.waiting = None


def cut(live, *flows):
    flows = [flow for flow in flows if not flow.done]
    sends = [
        flow.flying if flow.flying is not None else [item[0] for item in flow.waiting]
        for flow in flows
    ]
    live, sends = lax.optimization_barrier((live, sends))
    for flow, arrays in zip(flows, sends):
        if flow.flying is not None:
            flow.flying = None
            flow.advance(arrays)
        else:
            flow.waiting = [(a,) + item[1:] for a, item in zip(arrays, flow.waiting)]
        flow.launch()
    return live


def drain(live, *flows):
    while not all(flow.done for flow in flows):
        live = cut(live, *flows)
    return live


def grown(held, other, mask, flip=None):
    bit = bit_of("dp", mask)
    if flip is not None:
        bit = bit ^ flip
    joined = ordered(held, other, bit, -3)
    return joined.reshape(held.shape[:-3] + (-1,) + held.shape[-2:])


def gather_small(piece):
    held = piece[None]
    for mask in reversed(masks_of("dp")):
        (other,) = yield [(held, "dp", mask)]
        held = grown(held, other, mask)
    return held


def rows_of(held):
    return held.reshape(held.shape[:-3] + (-1, held.shape[-1]))


def quarter_of(block):
    width = block.shape[1] // 4
    start = (2 * lax.axis_index("uly") + lax.axis_index("blk")) * width
    return lax.dynamic_slice_in_dim(block, start, width, 1)


def gather_attention(first, second):
    held = jnp.stack([quarter_of(first), quarter_of(second)])[:, None]
    masks = masks_of("dp")
    held = yield from gather_far(held)
    for mask in reversed(masks[1:-2]):
        (other,) = yield [(held, "dp", mask)]
        held = grown(held, other, mask)
    left, right = held[0], held[1]
    place = bit_of("uly")
    other_left, other_right = yield [(left, "dp", masks[0]), (right, "uly", 1)]
    left = grown(left, other_left, masks[0])
    right = ordered(right, other_right, place, 0)
    other_left, other_right = yield [(left, "uly", 1), (right, "dp", masks[0])]
    left = rows_of(ordered(left, other_left, place, 0))
    right = rows_of(grown(right, other_right, masks[0]))
    other = yield [(left, "blk", 1), (right, "blk", 1)]
    return (left, right), tuple(other)


def gather_up(block):
    width = block.shape[1] // 4
    start = (2 * lax.axis_index("blk") + lax.axis_index("uly")) * width
    held = lax.dynamic_slice_in_dim(block, start, width, 1)[None]
    for mask in reversed(masks_of("dp")):
        (other,) = yield [(held, "dp", mask)]
        held = grown(held, other, mask)
    rows = rows_of(held)
    (other,) = yield [(rows, "uly", 1)]
    own = ordered(rows, other, bit_of("uly"), 0)
    (other,) = yield [(own, "blk", 1)]
    return own, other


def gather_down(block):
    width = block.shape[1] // 2
    held = lax.dynamic_slice_in_dim(block, lax.axis_index("blk") * width, width, 1)[None]
    masks = masks_of("dp")
    for mask in reversed(masks):
        (other,) = yield [(held, "dp", mask)]
        held = grown(held, other, mask, bit_of("blk") if mask == masks[-1] else None)
    own = held.reshape(2, -1, width)
    (other,) = yield [(own, "blk", 1)]
    return own, other


def halved(held, bit):
    return chosen(held, bit, -3), chosen(held, ~bit, -3)


def split_rows(held):
    return held.reshape(held.shape[:-3] + (-1, 2) + held.shape[-2:])


def reduce_attention(own, other):
    count = lax.axis_size("dp")
    masks = masks_of("dp")
    place = bit_of("uly")
    arrived = yield [(other[0], "blk", 1), (other[1], "blk", 1)]
    left, right = added(own[0], arrived[0]), added(own[1], arrived[1])
    two, rows, width = left.shape
    left = left.reshape(2, count, rows // count, width)
    right = right.reshape(2, count, rows // count, width)
    keep_left, send_left = chosen(left, place, 0), chosen(left, ~place, 0)
    bit = bit_of("dp", masks[0])
    keep_right, send_right = halved(split_rows(right), bit)
    arrived = yield [(send_left, "uly", 1), (send_right, "dp", masks[0])]
    left, right = added(keep_left, arrived[0]), added(keep_right, arrived[1])
    keep_left, send_left = halved(split_rows(left), bit)
    keep_right, send_right = chosen(right, place, 0), chosen(right, ~place, 0)
    arrived = yield [(send_left, "dp", masks[0]), (send_right, "uly", 1)]
    held = jnp.stack([added(keep_left, arrived[0]), added(keep_right, arrived[1])])
    for mask in masks[1:-2]:
        keep, send = halved(split_rows(held), bit_of("dp", mask))
        (other,) = yield [(send, "dp", mask)]
        held = added(keep, other)
    held = yield from reduce_far(held)
    return (yield from gather_partners(held))


def reduce_up(own, other):
    count = lax.axis_size("dp")
    place = bit_of("uly")
    (arrived,) = yield [(other, "blk", 1)]
    held = added(own, arrived)
    two, rows, width = held.shape
    keep, send = chosen(held, place, 0), chosen(held, ~place, 0)
    (arrived,) = yield [(send, "uly", 1)]
    held = added(keep, arrived).reshape(count, rows // count, width)
    for mask in masks_of("dp"):
        keep, send = halved(split_rows(held), bit_of("dp", mask))
        (arrived,) = yield [(send, "dp", mask)]
        held = added(keep, arrived)
    every = yield from gather_partners(held[0])
    return jnp.concatenate([every[i, j] for i in range(2) for j in range(2)], axis=-1)


def reduce_down(own, other):
    count = lax.axis_size("dp")
    masks = masks_of("dp")
    (arrived,) = yield [(other, "blk", 1)]
    held = added(own, jnp.stack([arrived[1], arrived[0]]))
    width = held.shape[2]
    held = held.reshape(count, -1, width)
    for mask in masks:
        bit = bit_of("dp", mask)
        if mask == masks[-1]:
            bit = bit ^ bit_of("blk")
        keep, send = halved(split_rows(held), bit)
        (arrived,) = yield [(send, "dp", mask)]
        held = added(keep, arrived)
    held = held[0]
    (arrived,) = yield [(held, "uly", 1)]
    held = added(held, arrived)
    (arrived,) = yield [(held, "blk", 1)]
    return side_by_side(held, arrived, bit_of("blk"))


def to_sequences(local):
    place = bit_of("uly")
    count, rows, width = local.shape
    paired = local.reshape(2, count // 2, rows, width)
    (arrived,) = yield [(chosen(paired, ~place, 0), "uly", 1)]
    joined = ordered(chosen(paired, place, 0), arrived, place, 1)
    return joined.reshape(count // 2, 2 * rows, width)


def from_sequences(held):
    place = bit_of("uly")
    count, rows, width = held.shape
    paired = held.reshape(count, 2, rows // 2, width)
    (arrived,) = yield [(chosen(paired, ~place, 1).astype(LOW), "uly", 1)]
    joined = ordered(chosen(paired, place, 1), arrived.astype(FULL), place, 0)
    return joined.reshape(2 * count, rows // 2, width)


def token_sum(item):
    return jnp.sum(item.astype(FULL), axis=(0, 1))[None]


def halves_of(item):
    half = item.shape[-1] // 2
    low, high = item[..., :half], item[..., half:]
    bit = bit_of("blk")
    return jnp.where(bit, high, low), jnp.where(bit, low, high)


def layer_forward(residual, small, flows, coming, core):
    attention, up_flow, down_flow = flows
    first_gain, first_shift, query_bias, value_bias, out_bias = (small[i : i + 1] for i in range(5))
    second_gain, second_shift, down_bias = (small[i : i + 1] for i in range(5, 8))
    bit = bit_of("blk")
    next_attention, next_up, next_down = coming if coming else (None, None, None)

    def with_next(*items):
        return [item for item in items if item is not None]

    own, other = attention.result
    normed = normalize(residual, first_gain, first_shift).astype(LOW)
    normed = cut(normed, up_flow, down_flow)
    query_biases, value_biases = halves_of(query_bias), halves_of(value_bias)

    def project(weights, i):
        (query, key), (value, unused) = weights
        return jnp.stack(
            [
                (matmul(normed, query) + query_biases[i]).astype(LOW),
                matmul(normed, key).astype(LOW),
                (matmul(normed, value) + value_biases[i]).astype(LOW),
            ]
        )

    away = swap(project(other, 1), "blk")
    mine = project(own, 0)
    mine, away = cut((mine, away), *with_next(next_attention))
    mixed_mine, mixed_theirs, logsum = attend(core, mine, away)
    mixed_mine, mixed_theirs = cut(
        (mixed_mine, mixed_theirs),
        up_flow,
        down_flow,
        *with_next(next_attention, next_up),
    )
    arrived = swap(mixed_theirs, "blk")
    mixed = side_by_side(mixed_mine, arrived, bit)
    columns = side_by_side(matmul(mixed, own[1][1]), matmul(mixed, other[1][1]), bit)
    middle = residual + columns + out_bias
    normed_two = normalize(middle, second_gain, second_shift).astype(LOW)
    middle, normed_two = cut(
        (middle, normed_two), up_flow, down_flow, *with_next(next_attention, next_up, next_down)
    )
    middle, normed_two = drain((middle, normed_two), up_flow)
    low_biases, high_biases = small[8:10], small[10:12]
    up_biases = jnp.where(bit, high_biases, low_biases), jnp.where(bit, low_biases, high_biases)
    hidden = []
    active = []
    for weights, bias in zip(up_flow.result, up_biases):
        parts = [
            matmul(normed_two, weights[i]) + bias[i : i + 1] for i in range(2)
        ]
        hidden.append(parts)
        active.append(jnp.concatenate([gelu(item).astype(LOW) for item in parts], axis=-1))
    active, middle = cut(
        (active, middle), down_flow, *with_next(next_attention, next_up, next_down)
    )
    active, middle = drain((active, middle), down_flow)
    down_own, down_other = down_flow.result
    left = matmul(active[0], down_own[0]) + matmul(active[1], down_own[1])
    right = matmul(active[0], down_other[1]) + matmul(active[1], down_other[0])
    result = middle + side_by_side(left, right, bit) + down_bias
    if coming:
        result = cut(result, next_attention)
    record = (residual, normed, mine, away, logsum, mixed_mine, mixed_theirs, mixed)
    return result, record + (middle, normed_two, hidden, active)


def layer_backward(upstream, small, weights, record, core, before, lowest):
    (own, other), (up_own, up_other), (down_own, down_other) = weights
    first_gain, second_gain = small[0:1], small[5:6]
    residual, normed, mine, away, logsum, mixed_mine, mixed_theirs, mixed = record[:8]
    middle, normed_two, hidden, active = record[8:]
    bit = bit_of("blk")

    down_bias_slope = token_sum(upstream)
    low_own, low_other = halves_of(upstream.astype(LOW))
    down_slopes = [
        jnp.stack([contract(active[i], low_other) for i in range(2)]),
        jnp.stack([contract(active[i], low_own) for i in range(2)]),
    ]
    down_flow = Flow(reduce_down(down_slopes[1], down_slopes[0]))
    low_own, low_other, upstream = cut((low_own, low_other, upstream), down_flow, *before[:2])
    active_slopes = [
        transposed(low_own, down_own[0]) + transposed(low_other, down_other[1]),
        transposed(low_own, down_own[1]) + transposed(low_other, down_other[0]),
    ]
    low_hidden = []
    bias_slopes = []
    for slope, parts in zip(active_slopes, hidden):
        width = parts[0].shape[-1]
        for i, item in enumerate(parts):
            unused, pullback = jax.vjp(gelu, item)
            hidden_slope = pullback(slope[..., i * width : (i + 1) * width])[0]
            bias_slopes.append(token_sum(hidden_slope))
            low_hidden.append(hidden_slope.astype(LOW))
    low_hidden = cut(low_hidden, down_flow, *before)
    low_biases = [jnp.where(bit, bias_slopes[2 + i], bias_slopes[i]) for i in range(2)]
    high_biases = [jnp.where(bit, bias_slopes[i], bias_slopes[2 + i]) for i in range(2)]
    up_slopes = [
        jnp.stack([contract(normed_two, low_hidden[2 + i]) for i in range(2)]),
        jnp.stack([contract(normed_two, low_hidden[i]) for i in range(2)]),
    ]
    up_flow = Flow(reduce_up(up_slopes[1], up_slopes[0]))
    low_hidden = cut(low_hidden, up_flow)
    norm_slope = (
        transposed(low_hidden[0], up_own[0])
        + transposed(low_hidden[1], up_own[1])
        + transposed(low_hidden[2], up_other[0])
        + transposed(low_hidden[3], up_other[1])
    )
    through, second_gain_slope, second_shift_slope = norm_backward(middle, second_gain, norm_slope)
    middle_slope = upstream + through
    middle_slope = cut(middle_slope, up_flow, *before)

    out_bias_slope = token_sum(middle_slope)
    low_own, low_other = halves_of(middle_slope.astype(LOW))
    mixed_slope = transposed(low_own, own[1][1]) + transposed(low_other, other[1][1])
    slope_own, slope_other = halves_of(mixed_slope.astype(LOW))
    slope_away = swap(slope_other, "blk")
    out_slopes = contract(mixed, low_own), contract(mixed, low_other)
    slope_own, slope_away, out_slopes = cut((slope_own, slope_away, out_slopes), *before)
    grads_mine, grads_theirs = attend_back(
        core, mine, away, logsum, (mixed_mine, mixed_theirs), (slope_own, slope_away)
    )
    grads_mine, grads_theirs, middle_slope = cut(
        (grads_mine, grads_theirs, middle_slope), down_flow, up_flow, *before
    )
    grads_away = swap(grads_theirs, "blk")
    first, second = [], []
    for grads, out_slope in zip((grads_mine, grads_away), out_slopes):
        slopes = [contract(normed, grads[i]) for i in range(3)]
        first.append(jnp.stack(slopes[:2]))
        second.append(jnp.stack([slopes[2], out_slope]))
    attention_flow = Flow(reduce_attention((first[0], second[0]), (first[1], second[1])))
    grads_mine, grads_away, middle_slope = cut(
        (grads_mine, grads_away, middle_slope),
        attention_flow,
        *before,
        *([down_flow] if lowest else []),
    )
    query_bias_slope = side_by_side(token_sum(grads_mine[0]), token_sum(grads_away[0]), bit)
    value_bias_slope = side_by_side(token_sum(grads_mine[2]), token_sum(grads_away[2]), bit)
    first_slope = 0.0
    for grads, (pair, last) in ((grads_mine, own), (grads_away, other)):
        first_slope = (
            first_slope
            + transposed(grads[0], pair[0])
            + transposed(grads[1], pair[1])
            + transposed(grads[2], last[0])
        )
    if lowest:
        first_slope = cut(first_slope, attention_flow)
    through, first_gain_slope, first_shift_slope = norm_backward(residual, first_gain, first_slope)
    upstream = middle_slope + through
    upstream = cut(upstream, attention_flow, up_flow, down_flow, *before)
    vectors = [
        first_gain_slope,
        first_shift_slope,
        query_bias_slope,
        value_bias_slope,
        out_bias_slope,
        second_gain_slope,
        second_shift_slope,
        down_bias_slope,
    ]
    terms = jnp.concatenate(vectors + low_biases + high_biases)
    return upstream, terms, (attention_flow, up_flow, down_flow)


def shards(
    inputs,
    cotangent,
    first_gain,
    first_shift,
    in_weight,
    query_bias,
    value_bias,
    out_weight,
    out_bias,
    second_gain,
    second_shift,
    up_weight,
    up_bias,
    down_weight,
    down_bias,
):
    layers, rows = in_weight.shape[0], in_weight.shape[1]
    width = out_weight.shape[2]
    core = lax.axis_index("blk").astype(jnp.int32).reshape(1)
    vectors = jnp.stack(
        [
            first_gain,
            first_shift,
            query_bias,
            value_bias,
            out_bias,
            second_gain,
            second_shift,
            down_bias,
        ],
        axis=1,
    )
    vectors = jnp.concatenate([vectors, up_bias.reshape(layers, -1, rows)], axis=1)
    kinds = vectors.shape[1]

    flows = []
    for layer in range(layers):
        first = in_weight[layer][:, : 2 * width]
        second = jnp.concatenate([in_weight[layer][:, 2 * width :], out_weight[layer]], axis=1)
        flows.append(
            (
                Flow(gather_attention(first, second)),
                Flow(gather_up(up_weight[layer])),
                Flow(gather_down(down_weight[layer])),
            )
        )
    attention, up_flow, down_flow = flows[0]
    entering = Flow(to_sequences(inputs))
    vector_flow = Flow(gather_small(vectors.reshape(layers * kinds, rows)))
    cut((), attention, entering, vector_flow)
    cut((), attention, entering, vector_flow, up_flow)
    residual = entering.result.astype(FULL)
    residual = cut(residual, attention, vector_flow, up_flow, down_flow)
    residual = drain(residual, vector_flow)
    gathered = vector_flow.result.reshape(-1, layers, kinds, rows).astype(FULL)
    straight = gathered.transpose(1, 2, 0, 3).reshape(layers, kinds, width)
    biases = gathered[:, :, 8:].transpose(1, 0, 2, 3).reshape(layers, kinds - 8, width)
    small = jnp.concatenate([straight[:, :8], biases], axis=1)
    residual = cut(residual, attention, up_flow, down_flow)
    leaving = Flow(to_sequences(cotangent))
    records = []
    for layer in range(layers):
        residual = drain(residual, flows[layer][0])
        coming = flows[layer + 1] if layer + 1 < layers else None
        if coming is None:
            residual = cut(residual, leaving)
        residual, record = layer_forward(residual, small[layer], flows[layer], coming, core)
        records.append(record)
    residual = drain(residual, leaving)
    outgoing = Flow(from_sequences(residual))
    upstream = leaving.result.astype(FULL)
    upstream = cut(upstream, outgoing)
    found = [None] * layers
    terms = [None] * layers
    before = ()
    for layer in reversed(range(layers)):
        weights = tuple(flow.result for flow in flows[layer])
        upstream, terms[layer], after = layer_backward(
            upstream, small[layer], weights, records[layer], core, before, layer == 0
        )
        upstream = drain(upstream, *before)
        before = after
        found[layer] = after
    gradient = Flow(from_sequences(upstream))
    totals = Flow(sum_small(jnp.concatenate(terms)))
    attention, up_flow, down_flow = before
    cut((), attention, down_flow, up_flow, totals, gradient)
    cut((), attention, up_flow, totals)
    drain((), *before, gradient, totals, outgoing)

    sums = totals.result.reshape(layers, kinds, width)
    place = lax.axis_index("dp")
    sliced = lax.dynamic_slice_in_dim(sums, place * rows, rows, 2)
    long = kinds - 8
    up_sums = lax.dynamic_slice_in_dim(
        sums[:, 8:].reshape(layers, -1), place * long * rows, long * rows, 1
    )
    matrices = [[], [], [], []]
    for layer in range(layers):
        attention, up_flow, down_flow = found[layer]
        pairs = attention.result
        whole = [
            jnp.concatenate([pairs[0, kind, block], pairs[1, kind, block]], axis=-1)
            for block in range(2)
            for kind in range(2)
        ]
        matrices[0].append(jnp.concatenate(whole[:3], axis=-1))
        matrices[1].append(whole[3])
        matrices[2].append(up_flow.result)
        matrices[3].append(down_flow.result)
    in_sum, out_sum, up_sum, down_sum = (jnp.stack(item).astype(FULL) for item in matrices)
    return (
        outgoing.result,
        gradient.result,
        sliced[:, 0],
        sliced[:, 1],
        in_sum,
        sliced[:, 2],
        sliced[:, 3],
        out_sum,
        sliced[:, 4],
        sliced[:, 5],
        sliced[:, 6],
        up_sum,
        up_sums,
        down_sum,
        sliced[:, 7],
    )


def solution(mesh):
    token = P("dp", ("blk", "uly"), None)
    vector = P(None, "dp")
    matrix = P(None, "dp", None)
    params = (
        vector,
        vector,
        matrix,
        vector,
        vector,
        matrix,
        vector,
        vector,
        vector,
        matrix,
        vector,
        matrix,
        vector,
    )
    specs = (token, token) + params
    return jax.shard_map(shards, mesh=mesh, in_specs=specs, out_specs=specs, check_vma=False)
```

```python
import jax
import jax.numpy as jnp
from jax import lax
from jax.experimental import pallas as pl
from jax.experimental.pallas import tpu as pltpu
from jax.sharding import PartitionSpec as P

HDIM = 64
EPSILON = 1e-05
NEGATIVE = -1e30
LOW = jnp.bfloat16
FULL = jnp.float32
SCALE = HDIM**-0.5
TILE = 256
MIB = 2**20


def dot_nt(left, right):
    return lax.dot_general(left, right, (((1,), (1,)), ((), ())), preferred_element_type=FULL)


def dot_nn(left, right):
    return lax.dot_general(left, right, (((1,), (0,)), ((), ())), preferred_element_type=FULL)


def head_lanes(item, head):
    lane = lax.broadcasted_iota(jnp.int32, item.shape, 1)
    return jnp.where((lane // HDIM) == head, item, jnp.zeros_like(item))


def keep_diagonal(scores):
    keys = lax.broadcasted_iota(jnp.int32, scores.shape, 0)
    rows = lax.broadcasted_iota(jnp.int32, scores.shape, 1)
    return jnp.where(keys <= rows, scores, NEGATIVE)


def join(core, mine, theirs, whole):
    half = mine.shape[0]

    @pl.when(core == 0)
    def _():
        whole[:half] = mine[...]
        whole[half:] = theirs[...]

    @pl.when(core != 0)
    def _():
        whole[:half] = theirs[...]
        whole[half:] = mine[...]


def part(core, whole, mine, theirs):
    half = mine.shape[0]

    @pl.when(core == 0)
    def _():
        mine[...] = whole[:half].astype(mine.dtype)
        theirs[...] = whole[half:].astype(theirs.dtype)

    @pl.when(core != 0)
    def _():
        theirs[...] = whole[:half].astype(theirs.dtype)
        mine[...] = whole[half:].astype(mine.dtype)


def attend_kernel(core_ref, mine_ref, theirs_ref, mixed_mine, mixed_theirs, logsum_ref, qkv, mixed_ref):
    core = core_ref[0]
    for kind in range(3):
        join(core, mine_ref.at[kind, 0], theirs_ref.at[kind, 0], qkv.at[kind])
    length = qkv.shape[1]
    values_t = qkv[2].T
    for start in range(0, length, TILE):
        rows = slice(start, start + TILE)
        queries = qkv[0, rows] * jnp.asarray(SCALE, LOW)
        outs = []
        for head in range(2):
            own = head_lanes(queries, head)
            scores = keep_diagonal(dot_nt(qkv[1, rows], own))
            top = jnp.max(scores, axis=0, keepdims=True)
            if start:
                early = dot_nt(qkv[1, :start], own)
                top = jnp.maximum(top, jnp.max(early, axis=0, keepdims=True))
            raised = jnp.exp(scores - top)
            total = jnp.sum(raised, axis=0, keepdims=True)
            mixed = dot_nn(values_t[:, rows], raised.astype(LOW))
            if start:
                raised = jnp.exp(early - top)
                total = total + jnp.sum(raised, axis=0, keepdims=True)
                mixed = mixed + dot_nn(values_t[:, :start], raised.astype(LOW))
            outs.append((mixed / total)[head * HDIM : (head + 1) * HDIM])
            logsum_ref[0, 0, head : head + 1, rows] = top + jnp.log(total)
        mixed_ref[rows] = jnp.concatenate(outs, axis=0).T.astype(LOW)
    part(core, mixed_ref, mixed_mine.at[0], mixed_theirs.at[0])


def attend(core, mine, theirs):
    three, count, rows, width = mine.shape
    pairs = width // 128
    wide = pl.BlockSpec((3, 1, rows, 128), lambda s, p, core: (0, s, 0, p))
    thin = pl.BlockSpec((1, rows, 128), lambda s, p, core: (s, 0, p))
    return pl.pallas_call(
        attend_kernel,
        grid_spec=pltpu.PrefetchScalarGridSpec(
            num_scalar_prefetch=1,
            grid=(count, pairs),
            in_specs=[wide, wide],
            out_specs=[
                thin,
                thin,
                pl.BlockSpec((1, 1, 8, 2 * rows), lambda s, p, core: (s, p, 0, 0)),
            ],
            scratch_shapes=[pltpu.VMEM((3, 2 * rows, 128), LOW), pltpu.VMEM((2 * rows, 128), LOW)],
        ),
        out_shape=[
            jax.ShapeDtypeStruct((count, rows, width), LOW),
            jax.ShapeDtypeStruct((count, rows, width), LOW),
            jax.ShapeDtypeStruct((count, pairs, 8, 2 * rows), FULL),
        ],
        compiler_params=pltpu.CompilerParams(vmem_limit_bytes=32 * MIB),
        name="attend",
    )(core, mine, theirs)


def attend_back_kernel(
    core_ref,
    mine_ref,
    theirs_ref,
    logsum_ref,
    mixed_mine,
    mixed_theirs,
    slope_mine,
    slope_theirs,
    out_mine,
    out_theirs,
    qkv,
    mixed_ref,
    slope_ref,
    grads,
):
    core = core_ref[0]
    for kind in range(3):
        join(core, mine_ref.at[kind, 0], theirs_ref.at[kind, 0], qkv.at[kind])
    join(core, mixed_mine.at[0], mixed_theirs.at[0], mixed_ref)
    join(core, slope_mine.at[0], slope_theirs.at[0], slope_ref)
    length = qkv.shape[1]
    keys_t = qkv[1].T * jnp.asarray(SCALE, LOW)
    product = (mixed_ref[...].astype(FULL) * slope_ref[...].astype(FULL)).T
    inner = [
        jnp.sum(product[h * HDIM : (h + 1) * HDIM], axis=0, keepdims=True) for h in range(2)
    ]
    for start in range(0, length, TILE):
        rows = slice(start, start + TILE)
        queries = qkv[0, rows] * jnp.asarray(SCALE, LOW)
        slope = slope_ref[rows]
        query_slopes = []
        for head in range(2):
            own = head_lanes(queries, head)
            own_slope = head_lanes(slope, head)
            logsum = logsum_ref[0, 0, head : head + 1, rows]
            query_slope = None
            for first in range(0, start + TILE, TILE):
                span = slice(first, first + TILE)
                scores = dot_nt(qkv[1, span], own)
                if first == start:
                    scores = keep_diagonal(scores)
                shares = jnp.exp(scores - logsum)
                against = dot_nt(qkv[2, span], own_slope)
                slopes = (shares * (against - inner[head][:, rows])).astype(LOW)
                value_slope = dot_nn(shares.astype(LOW), own_slope)
                key_slope = dot_nn(slopes, own)
                if first == start and head == 0:
                    grads[2, span] = value_slope
                    grads[1, span] = key_slope
                else:
                    grads[2, span] += value_slope
                    grads[1, span] += key_slope
                piece = dot_nn(keys_t[:, span], slopes)
                query_slope = piece if query_slope is None else query_slope + piece
            query_slopes.append(query_slope[head * HDIM : (head + 1) * HDIM])
        grads[0, rows] = jnp.concatenate(query_slopes, axis=0).T
    for kind in range(3):
        part(core, grads.at[kind], out_mine.at[kind, 0], out_theirs.at[kind, 0])


def attend_back(core, mine, theirs, logsum, mixed, slope):
    three, count, rows, width = mine.shape
    pairs = width // 128
    wide = pl.BlockSpec((3, 1, rows, 128), lambda s, p, core: (0, s, 0, p))
    thin = pl.BlockSpec((1, rows, 128), lambda s, p, core: (s, 0, p))
    sums = pl.BlockSpec((1, 1, 8, 2 * rows), lambda s, p, core: (s, p, 0, 0))
    return pl.pallas_call(
        attend_back_kernel,
        grid_spec=pltpu.PrefetchScalarGridSpec(
            num_scalar_prefetch=1,
            grid=(count, pairs),
            in_specs=[wide, wide, sums, thin, thin, thin, thin],
            out_specs=[wide, wide],
            scratch_shapes=[
                pltpu.VMEM((3, 2 * rows, 128), LOW),
                pltpu.VMEM((2 * rows, 128), LOW),
                pltpu.VMEM((2 * rows, 128), LOW),
                pltpu.VMEM((3, 2 * rows, 128), FULL),
            ],
        ),
        out_shape=[jax.ShapeDtypeStruct(mine.shape, LOW)] * 2,
        compiler_params=pltpu.CompilerParams(vmem_limit_bytes=32 * MIB),
        name="attend_back",
    )(core, mine, theirs, logsum, *mixed, *slope)


def normalize(residual, gain, shift):
    average = jnp.mean(residual, axis=-1, keepdims=True)
    centred = residual - average
    variance = jnp.mean(centred * centred, axis=-1, keepdims=True)
    return centred * lax.rsqrt(variance + EPSILON) * gain + shift


def norm_backward(residual, gain, slope):
    average = jnp.mean(residual, axis=-1, keepdims=True)
    centred = residual - average
    scale = lax.rsqrt(jnp.mean(centred * centred, axis=-1, keepdims=True) + EPSILON)
    unit = centred * scale
    raised = slope * gain
    along = jnp.mean(raised * unit, axis=-1, keepdims=True)
    level = jnp.mean(raised, axis=-1, keepdims=True)
    return scale * (raised - level - unit * along), token_sum(slope * unit), token_sum(slope)


def partners(item):
    return [(item, "uly", 1), (item, "blk", 1), (item, ("blk", "uly"), 3)]


def far_sends(items):
    near = masks_of("dp")[-2]
    return [(item, "dp", (i + 1) * near) for i, item in enumerate(items)]


def sum_small(held):
    arrived = yield partners(held)
    held = total(held, *arrived)
    for mask in masks_of("dp")[:-2]:
        arrived = yield [(held, "dp", mask)]
        held = total(held, *arrived)
    arrived = yield far_sends([held] * 3)
    return total(held, *arrived)


def gather_far(held):
    near, far = masks_of("dp")[-2:]
    first, second, both = yield far_sends([held] * 3)
    low = ordered(held, first, bit_of("dp", near), -3)
    high = ordered(second, both, bit_of("dp", near), -3)
    joined = ordered(low, high, bit_of("dp", far), -5)
    return joined.reshape(held.shape[:-3] + (4,) + held.shape[-2:])


def reduce_far(held):
    place = lax.axis_index("dp") // masks_of("dp")[-2]
    axis = held.ndim - 3
    parts = [lax.dynamic_index_in_dim(held, place ^ i, axis, keepdims=False) for i in range(4)]
    arrived = yield far_sends(parts[1:])
    return total(parts[0], *arrived)


def gather_partners(held):
    along, across, both = yield partners(held)
    place = bit_of("uly")
    return ordered(ordered(held, along, place, 0), ordered(across, both, place, 0), bit_of("blk"), 0)


def gelu(hidden):
    return jax.nn.gelu(hidden, approximate=True)


def matmul(left, right):
    return jnp.dot(left, right, preferred_element_type=FULL)


def contract(left, right):
    return jnp.einsum("std,ste->de", left, right, preferred_element_type=FULL).astype(LOW)


def transposed(left, right):
    return jnp.einsum("ste,de->std", left, right, preferred_element_type=FULL)


def swap(item, axis, mask=1):
    count = 4 if isinstance(axis, tuple) else lax.axis_size(axis)
    return lax.ppermute(item, axis, [(i, i ^ mask) for i in range(count)])


def bit_of(axis, mask=1):
    return (lax.axis_index(axis) & mask) != 0


def masks_of(axis):
    count = lax.axis_size(axis)
    masks = []
    mask = 1
    while mask < count:
        masks.append(mask)
        mask *= 2
    return masks


def ordered(own, other, bit, axis):
    low = jnp.where(bit, other, own)
    high = jnp.where(bit, own, other)
    return jnp.stack([low, high], axis=axis)


def side_by_side(own, other, bit):
    low = jnp.where(bit, other, own)
    high = jnp.where(bit, own, other)
    return jnp.concatenate([low, high], axis=-1)


def chosen(item, bit, axis):
    return lax.dynamic_index_in_dim(item, bit.astype(jnp.int32), axis, keepdims=False)


def total(*items):
    return sum(item.astype(FULL) for item in items).astype(items[0].dtype)


def added(left, right):
    return (left.astype(FULL) + right.astype(FULL)).astype(LOW)


class Flow:
    def __init__(self, steps):
        self.steps = steps
        self.result = None
        self.done = False
        self.flying = None
        self.waiting = None
        self.advance(None)

    def advance(self, arrived):
        try:
            self.waiting = self.steps.send(arrived)
        except StopIteration as stop:
            self.done = True
            self.waiting = None
            self.result = stop.value

    def launch(self):
        if not self.done:
            self.flying = [swap(*send) for send in self.waiting]
            self.waiting = None


def cut(live, *flows):
    flows = [flow for flow in flows if not flow.done]
    sends = [
        flow.flying if flow.flying is not None else [item[0] for item in flow.waiting]
        for flow in flows
    ]
    live, sends = lax.optimization_barrier((live, sends))
    for flow, arrays in zip(flows, sends):
        if flow.flying is not None:
            flow.flying = None
            flow.advance(arrays)
        else:
            flow.waiting = [(a,) + item[1:] for a, item in zip(arrays, flow.waiting)]
        flow.launch()
    return live


def drain(live, *flows):
    while not all(flow.done for flow in flows):
        live = cut(live, *flows)
    return live


def grown(held, other, mask, flip=None):
    bit = bit_of("dp", mask)
    if flip is not None:
        bit = bit ^ flip
    joined = ordered(held, other, bit, -3)
    return joined.reshape(held.shape[:-3] + (-1,) + held.shape[-2:])


def gather_small(piece):
    held = piece[None]
    for mask in reversed(masks_of("dp")):
        (other,) = yield [(held, "dp", mask)]
        held = grown(held, other, mask)
    return held


def rows_of(held):
    return held.reshape(held.shape[:-3] + (-1, held.shape[-1]))


def quarter_of(block):
    width = block.shape[1] // 4
    start = (2 * lax.axis_index("uly") + lax.axis_index("blk")) * width
    return lax.dynamic_slice_in_dim(block, start, width, 1)


def gather_attention(first, second):
    held = jnp.stack([quarter_of(first), quarter_of(second)])[:, None]
    masks = masks_of("dp")
    held = yield from gather_far(held)
    for mask in reversed(masks[1:-2]):
        (other,) = yield [(held, "dp", mask)]
        held = grown(held, other, mask)
    left, right = held[0], held[1]
    place = bit_of("uly")
    other_left, other_right = yield [(left, "dp", masks[0]), (right, "uly", 1)]
    left = grown(left, other_left, masks[0])
    right = ordered(right, other_right, place, 0)
    other_left, other_right = yield [(left, "uly", 1), (right, "dp", masks[0])]
    left = rows_of(ordered(left, other_left, place, 0))
    right = rows_of(grown(right, other_right, masks[0]))
    other = yield [(left, "blk", 1), (right, "blk", 1)]
    return (left, right), tuple(other)


def gather_up(block):
    width = block.shape[1] // 4
    start = (2 * lax.axis_index("blk") + lax.axis_index("uly")) * width
    held = lax.dynamic_slice_in_dim(block, start, width, 1)[None]
    for mask in reversed(masks_of("dp")):
        (other,) = yield [(held, "dp", mask)]
        held = grown(held, other, mask)
    rows = rows_of(held)
    (other,) = yield [(rows, "uly", 1)]
    own = ordered(rows, other, bit_of("uly"), 0)
    (other,) = yield [(own, "blk", 1)]
    return own, other


def gather_down(block):
    width = block.shape[1] // 2
    held = lax.dynamic_slice_in_dim(block, lax.axis_index("blk") * width, width, 1)[None]
    masks = masks_of("dp")
    for mask in reversed(masks):
        (other,) = yield [(held, "dp", mask)]
        held = grown(held, other, mask, bit_of("blk") if mask == masks[-1] else None)
    own = held.reshape(2, -1, width)
    (other,) = yield [(own, "blk", 1)]
    return own, other


def halved(held, bit):
    return chosen(held, bit, -3), chosen(held, ~bit, -3)


def split_rows(held):
    return held.reshape(held.shape[:-3] + (-1, 2) + held.shape[-2:])


def reduce_attention(own, other):
    count = lax.axis_size("dp")
    masks = masks_of("dp")
    place = bit_of("uly")
    arrived = yield [(other[0], "blk", 1), (other[1], "blk", 1)]
    left, right = added(own[0], arrived[0]), added(own[1], arrived[1])
    two, rows, width = left.shape
    left = left.reshape(2, count, rows // count, width)
    right = right.reshape(2, count, rows // count, width)
    keep_left, send_left = chosen(left, place, 0), chosen(left, ~place, 0)
    bit = bit_of("dp", masks[0])
    keep_right, send_right = halved(split_rows(right), bit)
    arrived = yield [(send_left, "uly", 1), (send_right, "dp", masks[0])]
    left, right = added(keep_left, arrived[0]), added(keep_right, arrived[1])
    keep_left, send_left = halved(split_rows(left), bit)
    keep_right, send_right = chosen(right, place, 0), chosen(right, ~place, 0)
    arrived = yield [(send_left, "dp", masks[0]), (send_right, "uly", 1)]
    held = jnp.stack([added(keep_left, arrived[0]), added(keep_right, arrived[1])])
    for mask in masks[1:-2]:
        keep, send = halved(split_rows(held), bit_of("dp", mask))
        (other,) = yield [(send, "dp", mask)]
        held = added(keep, other)
    held = yield from reduce_far(held)
    return (yield from gather_partners(held))


def reduce_up(own, other):
    count = lax.axis_size("dp")
    place = bit_of("uly")
    (arrived,) = yield [(other, "blk", 1)]
    held = added(own, arrived)
    two, rows, width = held.shape
    keep, send = chosen(held, place, 0), chosen(held, ~place, 0)
    (arrived,) = yield [(send, "uly", 1)]
    held = added(keep, arrived).reshape(count, rows // count, width)
    for mask in masks_of("dp"):
        keep, send = halved(split_rows(held), bit_of("dp", mask))
        (arrived,) = yield [(send, "dp", mask)]
        held = added(keep, arrived)
    every = yield from gather_partners(held[0])
    return jnp.concatenate([every[i, j] for i in range(2) for j in range(2)], axis=-1)


def reduce_down(own, other):
    count = lax.axis_size("dp")
    masks = masks_of("dp")
    (arrived,) = yield [(other, "blk", 1)]
    held = added(own, jnp.stack([arrived[1], arrived[0]]))
    width = held.shape[2]
    held = held.reshape(count, -1, width)
    for mask in masks:
        bit = bit_of("dp", mask)
        if mask == masks[-1]:
            bit = bit ^ bit_of("blk")
        keep, send = halved(split_rows(held), bit)
        (arrived,) = yield [(send, "dp", mask)]
        held = added(keep, arrived)
    held = held[0]
    (arrived,) = yield [(held, "uly", 1)]
    held = added(held, arrived)
    (arrived,) = yield [(held, "blk", 1)]
    return side_by_side(held, arrived, bit_of("blk"))


def to_sequences(local):
    place = bit_of("uly")
    count, rows, width = local.shape
    paired = local.reshape(2, count // 2, rows, width)
    (arrived,) = yield [(chosen(paired, ~place, 0), "uly", 1)]
    joined = ordered(chosen(paired, place, 0), arrived, place, 1)
    return joined.reshape(count // 2, 2 * rows, width)


def from_sequences(held):
    place = bit_of("uly")
    count, rows, width = held.shape
    paired = held.reshape(count, 2, rows // 2, width)
    (arrived,) = yield [(chosen(paired, ~place, 1).astype(LOW), "uly", 1)]
    joined = ordered(chosen(paired, place, 1), arrived.astype(FULL), place, 0)
    return joined.reshape(2 * count, rows // 2, width)


def token_sum(item):
    return jnp.sum(item.astype(FULL), axis=(0, 1))[None]


def halves_of(item):
    half = item.shape[-1] // 2
    low, high = item[..., :half], item[..., half:]
    bit = bit_of("blk")
    return jnp.where(bit, high, low), jnp.where(bit, low, high)


def layer_forward(residual, small, flows, coming, core):
    attention, up_flow, down_flow = flows
    first_gain, first_shift, query_bias, value_bias, out_bias = (small[i : i + 1] for i in range(5))
    second_gain, second_shift, down_bias = (small[i : i + 1] for i in range(5, 8))
    bit = bit_of("blk")
    next_attention, next_up, next_down = coming if coming else (None, None, None)

    def with_next(*items):
        return [item for item in items if item is not None]

    own, other = attention.result
    normed = normalize(residual, first_gain, first_shift).astype(LOW)
    query_biases, value_biases = halves_of(query_bias), halves_of(value_bias)

    def project(weights, i):
        (query, key), (value, unused) = weights
        return jnp.stack(
            [
                (matmul(normed, query) + query_biases[i]).astype(LOW),
                matmul(normed, key).astype(LOW),
                (matmul(normed, value) + value_biases[i]).astype(LOW),
            ]
        )

    theirs, normed = cut((project(other, 1), normed), up_flow, down_flow)
    away = swap(theirs, "blk")
    mine = project(own, 0)
    mine, away = cut((mine, away), *with_next(next_attention))
    mixed_mine, mixed_theirs, logsum = attend(core, mine, away)
    mixed_mine, mixed_theirs = cut(
        (mixed_mine, mixed_theirs),
        up_flow,
        down_flow,
        *with_next(next_attention, next_up),
    )
    arrived = swap(mixed_theirs, "blk")
    mixed = side_by_side(mixed_mine, arrived, bit)
    columns = side_by_side(matmul(mixed, own[1][1]), matmul(mixed, other[1][1]), bit)
    middle = residual + columns + out_bias
    normed_two = normalize(middle, second_gain, second_shift).astype(LOW)
    middle, normed_two = cut(
        (middle, normed_two), up_flow, down_flow, *with_next(next_attention, next_up, next_down)
    )
    middle, normed_two = drain((middle, normed_two), up_flow)
    low_biases, high_biases = small[8:10], small[10:12]
    up_biases = jnp.where(bit, high_biases, low_biases), jnp.where(bit, low_biases, high_biases)
    hidden = []
    active = []
    for weights, bias in zip(up_flow.result, up_biases):
        parts = [
            matmul(normed_two, weights[i]) + bias[i : i + 1] for i in range(2)
        ]
        hidden.append(parts)
        active.append(jnp.concatenate([gelu(item).astype(LOW) for item in parts], axis=-1))
    active, middle = cut(
        (active, middle), down_flow, *with_next(next_attention, next_up, next_down)
    )
    active, middle = drain((active, middle), down_flow)
    down_own, down_other = down_flow.result
    left = matmul(active[0], down_own[0]) + matmul(active[1], down_own[1])
    right = matmul(active[0], down_other[1]) + matmul(active[1], down_other[0])
    result = middle + side_by_side(left, right, bit) + down_bias
    if coming:
        result = cut(result, next_attention)
    record = (residual, normed, mine, away, logsum, mixed_mine, mixed_theirs, mixed)
    return result, record + (middle, normed_two, hidden, active)


def layer_backward(upstream, small, weights, record, core, before, lowest):
    (own, other), (up_own, up_other), (down_own, down_other) = weights
    first_gain, second_gain = small[0:1], small[5:6]
    residual, normed, mine, away, logsum, mixed_mine, mixed_theirs, mixed = record[:8]
    middle, normed_two, hidden, active = record[8:]
    bit = bit_of("blk")

    down_bias_slope = token_sum(upstream)
    low_own, low_other = halves_of(upstream.astype(LOW))
    down_slopes = [
        jnp.stack([contract(active[i], low_other) for i in range(2)]),
        jnp.stack([contract(active[i], low_own) for i in range(2)]),
    ]
    down_flow = Flow(reduce_down(down_slopes[1], down_slopes[0]))
    low_own, low_other, upstream = cut((low_own, low_other, upstream), down_flow, *before[:2])
    active_slopes = [
        transposed(low_own, down_own[0]) + transposed(low_other, down_other[1]),
        transposed(low_own, down_own[1]) + transposed(low_other, down_other[0]),
    ]
    low_hidden = []
    bias_slopes = []
    for slope, parts in zip(active_slopes, hidden):
        width = parts[0].shape[-1]
        for i, item in enumerate(parts):
            unused, pullback = jax.vjp(gelu, item)
            hidden_slope = pullback(slope[..., i * width : (i + 1) * width])[0]
            bias_slopes.append(token_sum(hidden_slope))
            low_hidden.append(hidden_slope.astype(LOW))
    low_hidden = cut(low_hidden, down_flow, *before)
    low_biases = [jnp.where(bit, bias_slopes[2 + i], bias_slopes[i]) for i in range(2)]
    high_biases = [jnp.where(bit, bias_slopes[i], bias_slopes[2 + i]) for i in range(2)]
    up_slopes = [
        jnp.stack([contract(normed_two, low_hidden[2 + i]) for i in range(2)]),
        jnp.stack([contract(normed_two, low_hidden[i]) for i in range(2)]),
    ]
    up_flow = Flow(reduce_up(up_slopes[1], up_slopes[0]))
    low_hidden = cut(low_hidden, up_flow)
    norm_slope = (
        transposed(low_hidden[0], up_own[0])
        + transposed(low_hidden[1], up_own[1])
        + transposed(low_hidden[2], up_other[0])
        + transposed(low_hidden[3], up_other[1])
    )
    through, second_gain_slope, second_shift_slope = norm_backward(middle, second_gain, norm_slope)
    middle_slope = upstream + through
    middle_slope = cut(middle_slope, up_flow, *before)

    out_bias_slope = token_sum(middle_slope)
    low_own, low_other = halves_of(middle_slope.astype(LOW))
    mixed_slope = transposed(low_own, own[1][1]) + transposed(low_other, other[1][1])
    slope_own, slope_other = halves_of(mixed_slope.astype(LOW))
    slope_away = swap(slope_other, "blk")
    out_slopes = contract(mixed, low_own), contract(mixed, low_other)
    slope_own, slope_away, out_slopes = cut((slope_own, slope_away, out_slopes), *before)
    grads_mine, grads_theirs = attend_back(
        core, mine, away, logsum, (mixed_mine, mixed_theirs), (slope_own, slope_away)
    )
    grads_mine, grads_theirs, middle_slope = cut(
        (grads_mine, grads_theirs, middle_slope), down_flow, up_flow, *before
    )
    grads_away = swap(grads_theirs, "blk")
    first, second = [], []
    for grads, out_slope in zip((grads_mine, grads_away), out_slopes):
        slopes = [contract(normed, grads[i]) for i in range(3)]
        first.append(jnp.stack(slopes[:2]))
        second.append(jnp.stack([slopes[2], out_slope]))
    attention_flow = Flow(reduce_attention((first[0], second[0]), (first[1], second[1])))
    grads_mine, grads_away, middle_slope = cut(
        (grads_mine, grads_away, middle_slope),
        attention_flow,
        *before,
    )
    query_bias_slope = side_by_side(token_sum(grads_mine[0]), token_sum(grads_away[0]), bit)
    value_bias_slope = side_by_side(token_sum(grads_mine[2]), token_sum(grads_away[2]), bit)
    first_slope = 0.0
    for grads, (pair, last) in ((grads_mine, own), (grads_away, other)):
        first_slope = (
            first_slope
            + transposed(grads[0], pair[0])
            + transposed(grads[1], pair[1])
            + transposed(grads[2], last[0])
        )
    if lowest:
        first_slope = cut(first_slope, attention_flow, down_flow)
    through, first_gain_slope, first_shift_slope = norm_backward(residual, first_gain, first_slope)
    upstream = middle_slope + through
    upstream = cut(upstream, attention_flow, up_flow, down_flow, *before)
    vectors = [
        first_gain_slope,
        first_shift_slope,
        query_bias_slope,
        value_bias_slope,
        out_bias_slope,
        second_gain_slope,
        second_shift_slope,
        down_bias_slope,
    ]
    terms = jnp.concatenate(vectors + low_biases + high_biases)
    return upstream, terms, (attention_flow, up_flow, down_flow)


def shards(
    inputs,
    cotangent,
    first_gain,
    first_shift,
    in_weight,
    query_bias,
    value_bias,
    out_weight,
    out_bias,
    second_gain,
    second_shift,
    up_weight,
    up_bias,
    down_weight,
    down_bias,
):
    layers, rows = in_weight.shape[0], in_weight.shape[1]
    width = out_weight.shape[2]
    core = lax.axis_index("blk").astype(jnp.int32).reshape(1)
    vectors = jnp.stack(
        [
            first_gain,
            first_shift,
            query_bias,
            value_bias,
            out_bias,
            second_gain,
            second_shift,
            down_bias,
        ],
        axis=1,
    )
    vectors = jnp.concatenate([vectors, up_bias.reshape(layers, -1, rows)], axis=1)
    kinds = vectors.shape[1]

    flows = []
    for layer in range(layers):
        first = in_weight[layer][:, : 2 * width]
        second = jnp.concatenate([in_weight[layer][:, 2 * width :], out_weight[layer]], axis=1)
        flows.append(
            (
                Flow(gather_attention(first, second)),
                Flow(gather_up(up_weight[layer])),
                Flow(gather_down(down_weight[layer])),
            )
        )
    attention, up_flow, down_flow = flows[0]
    entering = Flow(to_sequences(inputs))
    vector_flow = Flow(gather_small(vectors.reshape(layers * kinds, rows)))
    cut((), attention, entering, vector_flow)
    cut((), attention, entering, vector_flow, up_flow)
    residual = entering.result.astype(FULL)
    residual = cut(residual, attention, vector_flow, up_flow, down_flow)
    residual = drain(residual, vector_flow)
    gathered = vector_flow.result.reshape(-1, layers, kinds, rows).astype(FULL)
    straight = gathered.transpose(1, 2, 0, 3).reshape(layers, kinds, width)
    biases = gathered[:, :, 8:].transpose(1, 0, 2, 3).reshape(layers, kinds - 8, width)
    small = jnp.concatenate([straight[:, :8], biases], axis=1)
    residual = cut(residual, attention, up_flow, down_flow)
    leaving = Flow(to_sequences(cotangent))
    records = []
    for layer in range(layers):
        residual = drain(residual, flows[layer][0])
        coming = flows[layer + 1] if layer + 1 < layers else None
        if coming is None:
            residual = cut(residual, leaving)
        residual, record = layer_forward(residual, small[layer], flows[layer], coming, core)
        records.append(record)
    residual = drain(residual, leaving)
    outgoing = Flow(from_sequences(residual))
    upstream = leaving.result.astype(FULL)
    upstream = cut(upstream, outgoing)
    found = [None] * layers
    terms = [None] * layers
    before = ()
    for layer in reversed(range(layers)):
        weights = tuple(flow.result for flow in flows[layer])
        upstream, terms[layer], after = layer_backward(
            upstream, small[layer], weights, records[layer], core, before, layer == 0
        )
        upstream = drain(upstream, *before)
        before = after
        found[layer] = after
    gradient = Flow(from_sequences(upstream))
    totals = Flow(sum_small(jnp.concatenate(terms)))
    attention, up_flow, down_flow = before
    cut((), attention, down_flow, up_flow, totals, gradient)
    cut((), attention, up_flow, totals)
    drain((), *before, gradient, totals, outgoing)

    sums = totals.result.reshape(layers, kinds, width)
    place = lax.axis_index("dp")
    sliced = lax.dynamic_slice_in_dim(sums, place * rows, rows, 2)
    long = kinds - 8
    up_sums = lax.dynamic_slice_in_dim(
        sums[:, 8:].reshape(layers, -1), place * long * rows, long * rows, 1
    )
    matrices = [[], [], [], []]
    for layer in range(layers):
        attention, up_flow, down_flow = found[layer]
        pairs = attention.result
        whole = [
            jnp.concatenate([pairs[0, kind, block], pairs[1, kind, block]], axis=-1)
            for block in range(2)
            for kind in range(2)
        ]
        matrices[0].append(jnp.concatenate(whole[:3], axis=-1))
        matrices[1].append(whole[3])
        matrices[2].append(up_flow.result)
        matrices[3].append(down_flow.result)
    in_sum, out_sum, up_sum, down_sum = (jnp.stack(item).astype(FULL) for item in matrices)
    return (
        outgoing.result,
        gradient.result,
        sliced[:, 0],
        sliced[:, 1],
        in_sum,
        sliced[:, 2],
        sliced[:, 3],
        out_sum,
        sliced[:, 4],
        sliced[:, 5],
        sliced[:, 6],
        up_sum,
        up_sums,
        down_sum,
        sliced[:, 7],
    )


def solution(mesh):
    token = P("dp", ("blk", "uly"), None)
    vector = P(None, "dp")
    matrix = P(None, "dp", None)
    params = (
        vector,
        vector,
        matrix,
        vector,
        vector,
        matrix,
        vector,
        vector,
        vector,
        matrix,
        vector,
        matrix,
        vector,
    )
    specs = (token, token) + params
    return jax.shard_map(shards, mesh=mesh, in_specs=specs, out_specs=specs, check_vma=False)
```

```python
import jax
import jax.numpy as jnp
from jax import lax
from jax.experimental import pallas as pl
from jax.experimental.pallas import tpu as pltpu
from jax.sharding import PartitionSpec as P

HDIM = 64
EPSILON = 1e-05
NEGATIVE = -1e30
LOW = jnp.bfloat16
FULL = jnp.float32
SCALE = HDIM**-0.5
TILE = 256
MIB = 2**20


def dot_nt(left, right):
    return lax.dot_general(left, right, (((1,), (1,)), ((), ())), preferred_element_type=FULL)


def dot_nn(left, right):
    return lax.dot_general(left, right, (((1,), (0,)), ((), ())), preferred_element_type=FULL)


def head_lanes(item, head):
    lane = lax.broadcasted_iota(jnp.int32, item.shape, 1)
    return jnp.where((lane // HDIM) == head, item, jnp.zeros_like(item))


def keep_diagonal(scores):
    keys = lax.broadcasted_iota(jnp.int32, scores.shape, 0)
    rows = lax.broadcasted_iota(jnp.int32, scores.shape, 1)
    return jnp.where(keys <= rows, scores, NEGATIVE)


def join(core, mine, theirs, whole):
    half = mine.shape[0]

    @pl.when(core == 0)
    def _():
        whole[:half] = mine[...]
        whole[half:] = theirs[...]

    @pl.when(core != 0)
    def _():
        whole[:half] = theirs[...]
        whole[half:] = mine[...]


def part(core, whole, mine, theirs):
    half = mine.shape[0]

    @pl.when(core == 0)
    def _():
        mine[...] = whole[:half].astype(mine.dtype)
        theirs[...] = whole[half:].astype(theirs.dtype)

    @pl.when(core != 0)
    def _():
        theirs[...] = whole[:half].astype(theirs.dtype)
        mine[...] = whole[half:].astype(mine.dtype)


def attend_kernel(core_ref, mine_ref, theirs_ref, mixed_mine, mixed_theirs, logsum_ref, qkv, mixed_ref):
    core = core_ref[0]
    for kind in range(3):
        join(core, mine_ref.at[kind, 0], theirs_ref.at[kind, 0], qkv.at[kind])
    length = qkv.shape[1]
    values_t = qkv[2].T
    for start in range(0, length, TILE):
        rows = slice(start, start + TILE)
        queries = qkv[0, rows] * jnp.asarray(SCALE, LOW)
        outs = []
        for head in range(2):
            own = head_lanes(queries, head)
            scores = keep_diagonal(dot_nt(qkv[1, rows], own))
            top = jnp.max(scores, axis=0, keepdims=True)
            if start:
                early = dot_nt(qkv[1, :start], own)
                top = jnp.maximum(top, jnp.max(early, axis=0, keepdims=True))
            raised = jnp.exp(scores - top)
            total = jnp.sum(raised, axis=0, keepdims=True)
            mixed = dot_nn(values_t[:, rows], raised.astype(LOW))
            if start:
                raised = jnp.exp(early - top)
                total = total + jnp.sum(raised, axis=0, keepdims=True)
                mixed = mixed + dot_nn(values_t[:, :start], raised.astype(LOW))
            outs.append((mixed / total)[head * HDIM : (head + 1) * HDIM])
            logsum_ref[0, 0, head : head + 1, rows] = top + jnp.log(total)
        mixed_ref[rows] = jnp.concatenate(outs, axis=0).T.astype(LOW)
    part(core, mixed_ref, mixed_mine.at[0], mixed_theirs.at[0])


def attend(core, mine, theirs):
    three, count, rows, width = mine.shape
    pairs = width // 128
    wide = pl.BlockSpec((3, 1, rows, 128), lambda s, p, core: (0, s, 0, p))
    thin = pl.BlockSpec((1, rows, 128), lambda s, p, core: (s, 0, p))
    return pl.pallas_call(
        attend_kernel,
        grid_spec=pltpu.PrefetchScalarGridSpec(
            num_scalar_prefetch=1,
            grid=(count, pairs),
            in_specs=[wide, wide],
            out_specs=[
                thin,
                thin,
                pl.BlockSpec((1, 1, 8, 2 * rows), lambda s, p, core: (s, p, 0, 0)),
            ],
            scratch_shapes=[pltpu.VMEM((3, 2 * rows, 128), LOW), pltpu.VMEM((2 * rows, 128), LOW)],
        ),
        out_shape=[
            jax.ShapeDtypeStruct((count, rows, width), LOW),
            jax.ShapeDtypeStruct((count, rows, width), LOW),
            jax.ShapeDtypeStruct((count, pairs, 8, 2 * rows), FULL),
        ],
        compiler_params=pltpu.CompilerParams(vmem_limit_bytes=32 * MIB),
        name="attend",
    )(core, mine, theirs)


def attend_back_kernel(
    core_ref,
    mine_ref,
    theirs_ref,
    logsum_ref,
    mixed_mine,
    mixed_theirs,
    slope_mine,
    slope_theirs,
    out_mine,
    out_theirs,
    qkv,
    mixed_ref,
    slope_ref,
    grads,
):
    core = core_ref[0]
    for kind in range(3):
        join(core, mine_ref.at[kind, 0], theirs_ref.at[kind, 0], qkv.at[kind])
    join(core, mixed_mine.at[0], mixed_theirs.at[0], mixed_ref)
    join(core, slope_mine.at[0], slope_theirs.at[0], slope_ref)
    length = qkv.shape[1]
    keys_t = qkv[1].T * jnp.asarray(SCALE, LOW)
    product = (mixed_ref[...].astype(FULL) * slope_ref[...].astype(FULL)).T
    inner = [
        jnp.sum(product[h * HDIM : (h + 1) * HDIM], axis=0, keepdims=True) for h in range(2)
    ]
    for start in range(0, length, TILE):
        rows = slice(start, start + TILE)
        queries = qkv[0, rows] * jnp.asarray(SCALE, LOW)
        slope = slope_ref[rows]
        query_slopes = []
        for head in range(2):
            own = head_lanes(queries, head)
            own_slope = head_lanes(slope, head)
            logsum = logsum_ref[0, 0, head : head + 1, rows]
            query_slope = None
            for first in range(0, start + TILE, TILE):
                span = slice(first, first + TILE)
                scores = dot_nt(qkv[1, span], own)
                if first == start:
                    scores = keep_diagonal(scores)
                shares = jnp.exp(scores - logsum)
                against = dot_nt(qkv[2, span], own_slope)
                slopes = (shares * (against - inner[head][:, rows])).astype(LOW)
                value_slope = dot_nn(shares.astype(LOW), own_slope)
                key_slope = dot_nn(slopes, own)
                if first == start and head == 0:
                    grads[2, span] = value_slope
                    grads[1, span] = key_slope
                else:
                    grads[2, span] += value_slope
                    grads[1, span] += key_slope
                piece = dot_nn(keys_t[:, span], slopes)
                query_slope = piece if query_slope is None else query_slope + piece
            query_slopes.append(query_slope[head * HDIM : (head + 1) * HDIM])
        grads[0, rows] = jnp.concatenate(query_slopes, axis=0).T
    for kind in range(3):
        part(core, grads.at[kind], out_mine.at[kind, 0], out_theirs.at[kind, 0])


def attend_back(core, mine, theirs, logsum, mixed, slope):
    three, count, rows, width = mine.shape
    pairs = width // 128
    wide = pl.BlockSpec((3, 1, rows, 128), lambda s, p, core: (0, s, 0, p))
    thin = pl.BlockSpec((1, rows, 128), lambda s, p, core: (s, 0, p))
    sums = pl.BlockSpec((1, 1, 8, 2 * rows), lambda s, p, core: (s, p, 0, 0))
    return pl.pallas_call(
        attend_back_kernel,
        grid_spec=pltpu.PrefetchScalarGridSpec(
            num_scalar_prefetch=1,
            grid=(count, pairs),
            in_specs=[wide, wide, sums, thin, thin, thin, thin],
            out_specs=[wide, wide],
            scratch_shapes=[
                pltpu.VMEM((3, 2 * rows, 128), LOW),
                pltpu.VMEM((2 * rows, 128), LOW),
                pltpu.VMEM((2 * rows, 128), LOW),
                pltpu.VMEM((3, 2 * rows, 128), FULL),
            ],
        ),
        out_shape=[jax.ShapeDtypeStruct(mine.shape, LOW)] * 2,
        compiler_params=pltpu.CompilerParams(vmem_limit_bytes=32 * MIB),
        name="attend_back",
    )(core, mine, theirs, logsum, *mixed, *slope)


def normalize(residual, gain, shift):
    average = jnp.mean(residual, axis=-1, keepdims=True)
    centred = residual - average
    variance = jnp.mean(centred * centred, axis=-1, keepdims=True)
    return centred * lax.rsqrt(variance + EPSILON) * gain + shift


def norm_backward(residual, gain, slope):
    average = jnp.mean(residual, axis=-1, keepdims=True)
    centred = residual - average
    scale = lax.rsqrt(jnp.mean(centred * centred, axis=-1, keepdims=True) + EPSILON)
    unit = centred * scale
    raised = slope * gain
    along = jnp.mean(raised * unit, axis=-1, keepdims=True)
    level = jnp.mean(raised, axis=-1, keepdims=True)
    return scale * (raised - level - unit * along), token_sum(slope * unit), token_sum(slope)


def partners(item):
    return [(item, "uly", 1), (item, "blk", 1), (item, ("blk", "uly"), 3)]


def far_sends(items):
    near = masks_of("dp")[-2]
    return [(item, "dp", (i + 1) * near) for i, item in enumerate(items)]


def sum_small(held):
    arrived = yield partners(held)
    held = total(held, *arrived)
    for mask in masks_of("dp")[:-2]:
        arrived = yield [(held, "dp", mask)]
        held = total(held, *arrived)
    arrived = yield far_sends([held] * 3)
    return total(held, *arrived)


def gather_far(held):
    near, far = masks_of("dp")[-2:]
    first, second, both = yield far_sends([held] * 3)
    low = ordered(held, first, bit_of("dp", near), -3)
    high = ordered(second, both, bit_of("dp", near), -3)
    joined = ordered(low, high, bit_of("dp", far), -5)
    return joined.reshape(held.shape[:-3] + (4,) + held.shape[-2:])


def reduce_far(held):
    place = lax.axis_index("dp") // masks_of("dp")[-2]
    axis = held.ndim - 3
    parts = [lax.dynamic_index_in_dim(held, place ^ i, axis, keepdims=False) for i in range(4)]
    arrived = yield far_sends(parts[1:])
    return total(parts[0], *arrived)


def gather_partners(held):
    along, across, both = yield partners(held)
    place = bit_of("uly")
    return ordered(ordered(held, along, place, 0), ordered(across, both, place, 0), bit_of("blk"), 0)


def gelu(hidden):
    return jax.nn.gelu(hidden, approximate=True)


def matmul(left, right):
    return jnp.dot(left, right, preferred_element_type=FULL)


def contract(left, right):
    return jnp.einsum("std,ste->de", left, right, preferred_element_type=FULL).astype(LOW)


def transposed(left, right):
    return jnp.einsum("ste,de->std", left, right, preferred_element_type=FULL)


def swap(item, axis, mask=1):
    count = 4 if isinstance(axis, tuple) else lax.axis_size(axis)
    return lax.ppermute(item, axis, [(i, i ^ mask) for i in range(count)])


def bit_of(axis, mask=1):
    return (lax.axis_index(axis) & mask) != 0


def masks_of(axis):
    count = lax.axis_size(axis)
    masks = []
    mask = 1
    while mask < count:
        masks.append(mask)
        mask *= 2
    return masks


def ordered(own, other, bit, axis):
    low = jnp.where(bit, other, own)
    high = jnp.where(bit, own, other)
    return jnp.stack([low, high], axis=axis)


def side_by_side(own, other, bit):
    low = jnp.where(bit, other, own)
    high = jnp.where(bit, own, other)
    return jnp.concatenate([low, high], axis=-1)


def chosen(item, bit, axis):
    return lax.dynamic_index_in_dim(item, bit.astype(jnp.int32), axis, keepdims=False)


def total(*items):
    return sum(item.astype(FULL) for item in items).astype(items[0].dtype)


def added(left, right):
    return (left.astype(FULL) + right.astype(FULL)).astype(LOW)


class Flow:
    def __init__(self, steps):
        self.steps = steps
        self.result = None
        self.done = False
        self.flying = None
        self.waiting = None
        self.advance(None)

    def advance(self, arrived):
        try:
            self.waiting = self.steps.send(arrived)
        except StopIteration as stop:
            self.done = True
            self.waiting = None
            self.result = stop.value

    def launch(self):
        if not self.done:
            self.flying = [swap(*send) for send in self.waiting]
            self.waiting = None


def cut(live, *flows):
    flows = [flow for flow in flows if not flow.done]
    sends = [
        flow.flying if flow.flying is not None else [item[0] for item in flow.waiting]
        for flow in flows
    ]
    live, sends = lax.optimization_barrier((live, sends))
    for flow, arrays in zip(flows, sends):
        if flow.flying is not None:
            flow.flying = None
            flow.advance(arrays)
        else:
            flow.waiting = [(a,) + item[1:] for a, item in zip(arrays, flow.waiting)]
        flow.launch()
    return live


def drain(live, *flows):
    while not all(flow.done for flow in flows):
        live = cut(live, *flows)
    return live


def grown(held, other, mask, flip=None):
    bit = bit_of("dp", mask)
    if flip is not None:
        bit = bit ^ flip
    joined = ordered(held, other, bit, -3)
    return joined.reshape(held.shape[:-3] + (-1,) + held.shape[-2:])


def gather_small(piece):
    held = piece[None]
    for mask in reversed(masks_of("dp")):
        (other,) = yield [(held, "dp", mask)]
        held = grown(held, other, mask)
    return held


def rows_of(held):
    return held.reshape(held.shape[:-3] + (-1, held.shape[-1]))


def quarter_of(block):
    width = block.shape[1] // 4
    start = (2 * lax.axis_index("uly") + lax.axis_index("blk")) * width
    return lax.dynamic_slice_in_dim(block, start, width, 1)


def gather_attention(first, second):
    held = jnp.stack([quarter_of(first), quarter_of(second)])[:, None]
    masks = masks_of("dp")
    held = yield from gather_far(held)
    for mask in reversed(masks[1:-2]):
        (other,) = yield [(held, "dp", mask)]
        held = grown(held, other, mask)
    left, right = held[0], held[1]
    place = bit_of("uly")
    other_left, other_right = yield [(left, "dp", masks[0]), (right, "uly", 1)]
    left = grown(left, other_left, masks[0])
    right = ordered(right, other_right, place, 0)
    other_left, other_right = yield [(left, "uly", 1), (right, "dp", masks[0])]
    left = rows_of(ordered(left, other_left, place, 0))
    right = rows_of(grown(right, other_right, masks[0]))
    other = yield [(left, "blk", 1), (right, "blk", 1)]
    return (left, right), tuple(other)


def gather_up(block):
    width = block.shape[1] // 4
    start = (2 * lax.axis_index("blk") + lax.axis_index("uly")) * width
    held = lax.dynamic_slice_in_dim(block, start, width, 1)[None]
    for mask in reversed(masks_of("dp")):
        (other,) = yield [(held, "dp", mask)]
        held = grown(held, other, mask)
    rows = rows_of(held)
    (other,) = yield [(rows, "uly", 1)]
    own = ordered(rows, other, bit_of("uly"), 0)
    (other,) = yield [(own, "blk", 1)]
    return own, other


def gather_down(block):
    width = block.shape[1] // 2
    held = lax.dynamic_slice_in_dim(block, lax.axis_index("blk") * width, width, 1)[None]
    masks = masks_of("dp")
    for mask in reversed(masks):
        (other,) = yield [(held, "dp", mask)]
        held = grown(held, other, mask, bit_of("blk") if mask == masks[-1] else None)
    own = held.reshape(2, -1, width)
    (other,) = yield [(own, "blk", 1)]
    return own, other


def halved(held, bit):
    return chosen(held, bit, -3), chosen(held, ~bit, -3)


def split_rows(held):
    return held.reshape(held.shape[:-3] + (-1, 2) + held.shape[-2:])


def reduce_attention(own, other):
    count = lax.axis_size("dp")
    masks = masks_of("dp")
    place = bit_of("uly")
    arrived = yield [(other[0], "blk", 1), (other[1], "blk", 1)]
    left, right = added(own[0], arrived[0]), added(own[1], arrived[1])
    two, rows, width = left.shape
    left = left.reshape(2, count, rows // count, width)
    right = right.reshape(2, count, rows // count, width)
    keep_left, send_left = chosen(left, place, 0), chosen(left, ~place, 0)
    bit = bit_of("dp", masks[0])
    keep_right, send_right = halved(split_rows(right), bit)
    arrived = yield [(send_left, "uly", 1), (send_right, "dp", masks[0])]
    left, right = added(keep_left, arrived[0]), added(keep_right, arrived[1])
    keep_left, send_left = halved(split_rows(left), bit)
    keep_right, send_right = chosen(right, place, 0), chosen(right, ~place, 0)
    arrived = yield [(send_left, "dp", masks[0]), (send_right, "uly", 1)]
    held = jnp.stack([added(keep_left, arrived[0]), added(keep_right, arrived[1])])
    for mask in masks[1:-2]:
        keep, send = halved(split_rows(held), bit_of("dp", mask))
        (other,) = yield [(send, "dp", mask)]
        held = added(keep, other)
    held = yield from reduce_far(held)
    return (yield from gather_partners(held))


def reduce_up(own, other):
    count = lax.axis_size("dp")
    place = bit_of("uly")
    (arrived,) = yield [(other, "blk", 1)]
    held = added(own, arrived)
    two, rows, width = held.shape
    keep, send = chosen(held, place, 0), chosen(held, ~place, 0)
    (arrived,) = yield [(send, "uly", 1)]
    held = added(keep, arrived).reshape(count, rows // count, width)
    for mask in masks_of("dp"):
        keep, send = halved(split_rows(held), bit_of("dp", mask))
        (arrived,) = yield [(send, "dp", mask)]
        held = added(keep, arrived)
    every = yield from gather_partners(held[0])
    return jnp.concatenate([every[i, j] for i in range(2) for j in range(2)], axis=-1)


def reduce_down(own, other):
    count = lax.axis_size("dp")
    masks = masks_of("dp")
    (arrived,) = yield [(other, "blk", 1)]
    held = added(own, jnp.stack([arrived[1], arrived[0]]))
    width = held.shape[2]
    held = held.reshape(count, -1, width)
    for mask in masks:
        bit = bit_of("dp", mask)
        if mask == masks[-1]:
            bit = bit ^ bit_of("blk")
        keep, send = halved(split_rows(held), bit)
        (arrived,) = yield [(send, "dp", mask)]
        held = added(keep, arrived)
    held = held[0]
    (arrived,) = yield [(held, "uly", 1)]
    held = added(held, arrived)
    (arrived,) = yield [(held, "blk", 1)]
    return side_by_side(held, arrived, bit_of("blk"))


def to_sequences(local):
    place = bit_of("uly")
    count, rows, width = local.shape
    paired = local.reshape(2, count // 2, rows, width)
    (arrived,) = yield [(chosen(paired, ~place, 0), "uly", 1)]
    joined = ordered(chosen(paired, place, 0), arrived, place, 1)
    return joined.reshape(count // 2, 2 * rows, width)


def from_sequences(held):
    place = bit_of("uly")
    count, rows, width = held.shape
    paired = held.reshape(count, 2, rows // 2, width)
    (arrived,) = yield [(chosen(paired, ~place, 1).astype(LOW), "uly", 1)]
    joined = ordered(chosen(paired, place, 1), arrived.astype(FULL), place, 0)
    return joined.reshape(2 * count, rows // 2, width)


def token_sum(item):
    return jnp.sum(item.astype(FULL), axis=(0, 1))[None]


def halves_of(item):
    half = item.shape[-1] // 2
    low, high = item[..., :half], item[..., half:]
    bit = bit_of("blk")
    return jnp.where(bit, high, low), jnp.where(bit, low, high)


def layer_forward(residual, small, flows, coming, core):
    attention, up_flow, down_flow = flows
    first_gain, first_shift, query_bias, value_bias, out_bias = (small[i : i + 1] for i in range(5))
    second_gain, second_shift, down_bias = (small[i : i + 1] for i in range(5, 8))
    bit = bit_of("blk")
    next_attention, next_up, next_down = coming if coming else (None, None, None)

    def with_next(*items):
        return [item for item in items if item is not None]

    own, other = attention.result
    normed = normalize(residual, first_gain, first_shift).astype(LOW)
    query_biases, value_biases = halves_of(query_bias), halves_of(value_bias)

    def project(weights, i):
        (query, key), (value, unused) = weights
        return jnp.stack(
            [
                (matmul(normed, query) + query_biases[i]).astype(LOW),
                matmul(normed, key).astype(LOW),
                (matmul(normed, value) + value_biases[i]).astype(LOW),
            ]
        )

    theirs, normed = cut((project(other, 1), normed), up_flow, down_flow)
    away = swap(theirs, "blk")
    mine = project(own, 0)
    mine, away = cut((mine, away), *with_next(next_attention))
    mixed_mine, mixed_theirs, logsum = attend(core, mine, away)
    mixed_mine, mixed_theirs = cut(
        (mixed_mine, mixed_theirs),
        up_flow,
        down_flow,
        *with_next(next_attention, next_up),
    )
    arrived = swap(mixed_theirs, "blk")
    mixed = side_by_side(mixed_mine, arrived, bit)
    columns = side_by_side(matmul(mixed, own[1][1]), matmul(mixed, other[1][1]), bit)
    middle = residual + columns + out_bias
    normed_two = normalize(middle, second_gain, second_shift).astype(LOW)
    middle, normed_two = cut(
        (middle, normed_two), up_flow, down_flow, *with_next(next_attention, next_up, next_down)
    )
    middle, normed_two = drain((middle, normed_two), up_flow)
    low_biases, high_biases = small[8:10], small[10:12]
    up_biases = jnp.where(bit, high_biases, low_biases), jnp.where(bit, low_biases, high_biases)
    hidden = []
    active = []
    for weights, bias in zip(up_flow.result, up_biases):
        parts = [
            matmul(normed_two, weights[i]) + bias[i : i + 1] for i in range(2)
        ]
        hidden.append(parts)
        active.append(jnp.concatenate([gelu(item).astype(LOW) for item in parts], axis=-1))
    active, middle = cut(
        (active, middle), down_flow, *with_next(next_attention, next_up, next_down)
    )
    active, middle = drain((active, middle), down_flow)
    down_own, down_other = down_flow.result
    left = matmul(active[0], down_own[0]) + matmul(active[1], down_own[1])
    right = matmul(active[0], down_other[1]) + matmul(active[1], down_other[0])
    result = middle + side_by_side(left, right, bit) + down_bias
    if coming:
        result = cut(result, next_attention)
    record = (residual, normed, mine, away, logsum, mixed_mine, mixed_theirs, mixed)
    return result, record + (middle, normed_two, hidden, active)


def layer_backward(upstream, small, weights, record, core, before, lowest):
    (own, other), (up_own, up_other), (down_own, down_other) = weights
    first_gain, second_gain = small[0:1], small[5:6]
    residual, normed, mine, away, logsum, mixed_mine, mixed_theirs, mixed = record[:8]
    middle, normed_two, hidden, active = record[8:]
    bit = bit_of("blk")

    down_bias_slope = token_sum(upstream)
    low_own, low_other = halves_of(upstream.astype(LOW))
    down_slopes = [
        jnp.stack([contract(active[i], low_other) for i in range(2)]),
        jnp.stack([contract(active[i], low_own) for i in range(2)]),
    ]
    down_flow = Flow(reduce_down(down_slopes[1], down_slopes[0]))
    low_own, low_other, upstream = cut((low_own, low_other, upstream), down_flow, *before[:2])
    active_slopes = [
        transposed(low_own, down_own[0]) + transposed(low_other, down_other[1]),
        transposed(low_own, down_own[1]) + transposed(low_other, down_other[0]),
    ]
    low_hidden = []
    bias_slopes = []
    for slope, parts in zip(active_slopes, hidden):
        width = parts[0].shape[-1]
        for i, item in enumerate(parts):
            unused, pullback = jax.vjp(gelu, item)
            hidden_slope = pullback(slope[..., i * width : (i + 1) * width])[0]
            bias_slopes.append(token_sum(hidden_slope))
            low_hidden.append(hidden_slope.astype(LOW))
    low_hidden = cut(low_hidden, down_flow, *before)
    low_biases = [jnp.where(bit, bias_slopes[2 + i], bias_slopes[i]) for i in range(2)]
    high_biases = [jnp.where(bit, bias_slopes[i], bias_slopes[2 + i]) for i in range(2)]
    up_slopes = [
        jnp.stack([contract(normed_two, low_hidden[2 + i]) for i in range(2)]),
        jnp.stack([contract(normed_two, low_hidden[i]) for i in range(2)]),
    ]
    up_flow = Flow(reduce_up(up_slopes[1], up_slopes[0]))
    low_hidden = cut(low_hidden, up_flow)
    norm_slope = (
        transposed(low_hidden[0], up_own[0])
        + transposed(low_hidden[1], up_own[1])
        + transposed(low_hidden[2], up_other[0])
        + transposed(low_hidden[3], up_other[1])
    )
    through, second_gain_slope, second_shift_slope = norm_backward(middle, second_gain, norm_slope)
    middle_slope = upstream + through
    middle_slope = cut(middle_slope, up_flow, *before)

    out_bias_slope = token_sum(middle_slope)
    low_own, low_other = halves_of(middle_slope.astype(LOW))
    mixed_slope = transposed(low_own, own[1][1]) + transposed(low_other, other[1][1])
    slope_own, slope_other = halves_of(mixed_slope.astype(LOW))
    slope_away = swap(slope_other, "blk")
    out_slopes = contract(mixed, low_own), contract(mixed, low_other)
    slope_own, slope_away, out_slopes = cut((slope_own, slope_away, out_slopes), *before)
    grads_mine, grads_theirs = attend_back(
        core, mine, away, logsum, (mixed_mine, mixed_theirs), (slope_own, slope_away)
    )
    grads_away = swap(grads_theirs, "blk")
    slopes_mine = [contract(normed, grads_mine[i]) for i in range(3)]
    grads_mine, grads_away, slopes_mine, middle_slope = cut(
        (grads_mine, grads_away, slopes_mine, middle_slope), down_flow, up_flow, *before
    )
    slopes_away = [contract(normed, grads_away[i]) for i in range(3)]
    first, second = [], []
    for slopes, out_slope in zip((slopes_mine, slopes_away), out_slopes):
        first.append(jnp.stack(slopes[:2]))
        second.append(jnp.stack([slopes[2], out_slope]))
    attention_flow = Flow(reduce_attention((first[0], second[0]), (first[1], second[1])))
    grads_mine, grads_away, middle_slope = cut(
        (grads_mine, grads_away, middle_slope),
        attention_flow,
        *before,
    )
    query_bias_slope = side_by_side(token_sum(grads_mine[0]), token_sum(grads_away[0]), bit)
    value_bias_slope = side_by_side(token_sum(grads_mine[2]), token_sum(grads_away[2]), bit)
    first_slope = 0.0
    for grads, (pair, last) in ((grads_mine, own), (grads_away, other)):
        first_slope = (
            first_slope
            + transposed(grads[0], pair[0])
            + transposed(grads[1], pair[1])
            + transposed(grads[2], last[0])
        )
    if lowest:
        first_slope = cut(first_slope, attention_flow, down_flow)
    through, first_gain_slope, first_shift_slope = norm_backward(residual, first_gain, first_slope)
    upstream = middle_slope + through
    upstream = cut(upstream, attention_flow, up_flow, down_flow, *before)
    vectors = [
        first_gain_slope,
        first_shift_slope,
        query_bias_slope,
        value_bias_slope,
        out_bias_slope,
        second_gain_slope,
        second_shift_slope,
        down_bias_slope,
    ]
    terms = jnp.concatenate(vectors + low_biases + high_biases)
    return upstream, terms, (attention_flow, up_flow, down_flow)


def shards(
    inputs,
    cotangent,
    first_gain,
    first_shift,
    in_weight,
    query_bias,
    value_bias,
    out_weight,
    out_bias,
    second_gain,
    second_shift,
    up_weight,
    up_bias,
    down_weight,
    down_bias,
):
    layers, rows = in_weight.shape[0], in_weight.shape[1]
    width = out_weight.shape[2]
    core = lax.axis_index("blk").astype(jnp.int32).reshape(1)
    vectors = jnp.stack(
        [
            first_gain,
            first_shift,
            query_bias,
            value_bias,
            out_bias,
            second_gain,
            second_shift,
            down_bias,
        ],
        axis=1,
    )
    vectors = jnp.concatenate([vectors, up_bias.reshape(layers, -1, rows)], axis=1)
    kinds = vectors.shape[1]

    flows = []
    for layer in range(layers):
        first = in_weight[layer][:, : 2 * width]
        second = jnp.concatenate([in_weight[layer][:, 2 * width :], out_weight[layer]], axis=1)
        flows.append(
            (
                Flow(gather_attention(first, second)),
                Flow(gather_up(up_weight[layer])),
                Flow(gather_down(down_weight[layer])),
            )
        )
    attention, up_flow, down_flow = flows[0]
    entering = Flow(to_sequences(inputs))
    vector_flow = Flow(gather_small(vectors.reshape(layers * kinds, rows)))
    cut((), attention, entering, vector_flow)
    cut((), attention, entering, vector_flow, up_flow)
    residual = entering.result.astype(FULL)
    residual = cut(residual, attention, vector_flow, up_flow, down_flow)
    residual = drain(residual, vector_flow)
    gathered = vector_flow.result.reshape(-1, layers, kinds, rows).astype(FULL)
    straight = gathered.transpose(1, 2, 0, 3).reshape(layers, kinds, width)
    biases = gathered[:, :, 8:].transpose(1, 0, 2, 3).reshape(layers, kinds - 8, width)
    small = jnp.concatenate([straight[:, :8], biases], axis=1)
    residual = cut(residual, attention, up_flow, down_flow)
    leaving = Flow(to_sequences(cotangent))
    records = []
    for layer in range(layers):
        residual = drain(residual, flows[layer][0])
        coming = flows[layer + 1] if layer + 1 < layers else None
        if coming is None:
            residual = cut(residual, leaving)
        residual, record = layer_forward(residual, small[layer], flows[layer], coming, core)
        records.append(record)
    residual = drain(residual, leaving)
    outgoing = Flow(from_sequences(residual))
    upstream = leaving.result.astype(FULL)
    upstream = cut(upstream, outgoing)
    found = [None] * layers
    terms = [None] * layers
    before = ()
    for layer in reversed(range(layers)):
        weights = tuple(flow.result for flow in flows[layer])
        upstream, terms[layer], after = layer_backward(
            upstream, small[layer], weights, records[layer], core, before, layer == 0
        )
        upstream = drain(upstream, *before)
        before = after
        found[layer] = after
    gradient = Flow(from_sequences(upstream))
    totals = Flow(sum_small(jnp.concatenate(terms)))
    attention, up_flow, down_flow = before
    cut((), attention, down_flow, up_flow, totals, gradient)
    cut((), attention, up_flow, totals)
    drain((), *before, gradient, totals, outgoing)

    sums = totals.result.reshape(layers, kinds, width)
    place = lax.axis_index("dp")
    sliced = lax.dynamic_slice_in_dim(sums, place * rows, rows, 2)
    long = kinds - 8
    up_sums = lax.dynamic_slice_in_dim(
        sums[:, 8:].reshape(layers, -1), place * long * rows, long * rows, 1
    )
    matrices = [[], [], [], []]
    for layer in range(layers):
        attention, up_flow, down_flow = found[layer]
        pairs = attention.result
        whole = [
            jnp.concatenate([pairs[0, kind, block], pairs[1, kind, block]], axis=-1)
            for block in range(2)
            for kind in range(2)
        ]
        matrices[0].append(jnp.concatenate(whole[:3], axis=-1))
        matrices[1].append(whole[3])
        matrices[2].append(up_flow.result)
        matrices[3].append(down_flow.result)
    in_sum, out_sum, up_sum, down_sum = (jnp.stack(item).astype(FULL) for item in matrices)
    return (
        outgoing.result,
        gradient.result,
        sliced[:, 0],
        sliced[:, 1],
        in_sum,
        sliced[:, 2],
        sliced[:, 3],
        out_sum,
        sliced[:, 4],
        sliced[:, 5],
        sliced[:, 6],
        up_sum,
        up_sums,
        down_sum,
        sliced[:, 7],
    )


def solution(mesh):
    token = P("dp", ("blk", "uly"), None)
    vector = P(None, "dp")
    matrix = P(None, "dp", None)
    params = (
        vector,
        vector,
        matrix,
        vector,
        vector,
        matrix,
        vector,
        vector,
        vector,
        matrix,
        vector,
        matrix,
        vector,
    )
    specs = (token, token) + params
    return jax.shard_map(shards, mesh=mesh, in_specs=specs, out_specs=specs, check_vma=False)
```
